256 devices in a mesh: sec: 64 (over x, z, core), strip: 4 (over y).
Axes of the slice: x: 4, y: 4, z: 8, core: 2. Of those that a mesh axis runs over, the one named last changes fastest.
Arguments:
- features: bfloat16 [128, 8, 32, 160, 160], P('sec', 'strip'), may hold values from -6 to 6
- intersection: int32 [128, 4, 2], P('sec', 'strip'), may hold values from 0 to 1, each once within a row
- peak_offsets: int32 [128, 8, 2], P('sec', 'strip'), may hold values from -12 to 12
- node_valid: int32 [128, 8], P('sec', 'strip'), may hold values 0 or 1
Outputs:
- scores: float32 [128, 8, 5], P('sec', 'strip')
- positions: float32 [128, 8, 2], P('sec', 'strip')
The draws below stay inside these ranges and needn't reach their ends.
Inputs may be any that keep to these rules, and one draw needn't show every extreme that they name: `intersection`: each row of 2 entries names every patch of the strip once.
All inputs are finite; a program needn't handle non-finite values. No bound on the sum of `node_valid` on one device may be relied on, other than what follows from the above.
Results may differ from the reference program's by a relative error of at most 0.0076.
Values may be sent and summed in bfloat16 or wider, within the bound.
No kernel may reach another device: no remote copies, remote signals or barrier semaphores. Data moves between devices by JAX's collectives and lax.ppermute only.
A program may use at most 192 MiB of HBM per device.

```python
import math
import jax
import jax.numpy as jnp
from jax import lax

C = 32
W = 160
P_SIZE = 2
ITERS = 8
STRIPS = 4
SECTIONS = 128
PATCHES = 8


def with_ends(result, stream_key, smallest, largest):
    place = [jax.random.randint(jax.random.fold_in(stream_key, axis), (), 0, length) for axis, length in enumerate(result.shape)]
    main_axis = result.shape.index(max(result.shape))
    neighbour = place[:main_axis] + [(place[main_axis] + 1) % result.shape[main_axis]] + place[main_axis + 1:]
    return result.at[tuple(place)].set(smallest).at[tuple(neighbour)].set(largest)


def steps_of(rng, extent, shards, low, top_value):
    def one(position, parts):
        steps = jax.random.uniform(jax.random.fold_in(jax.random.fold_in(rng, 6), position), (parts,), jnp.float32, low / len(shards), top_value / len(shards))
        return jnp.repeat(jnp.exp(steps), extent[position] // parts).reshape((-1,) + (1,) * (len(extent) - position - 1))

    loudness = one(*shards[0])
    for cut in shards[1:]:
        loudness = loudness * one(*cut)
    return loudness


def scatter_about(stream_key, shape, scale, reach, shards=(), held_as=jnp.bfloat16):
    result = scale * jax.random.normal(stream_key, shape, jnp.float32)
    if shards:
        result = result * steps_of(stream_key, shape, shards, -0.22, 0.18)
    return jnp.clip(result, -reach, reach).astype(held_as)


def setup_inputs(seed: int = 0) -> dict:
    seeds = jax.random.split(jax.random.key(seed), 5)
    features = scatter_about(seeds[0], (SECTIONS, PATCHES, C, W, W), 1.0, 6.0, ((0, 64), (1, 4)))
    intersection = jax.vmap(lambda own: jax.random.permutation(own, P_SIZE))(jax.random.split(seeds[1], SECTIONS * STRIPS)).reshape((SECTIONS, STRIPS, P_SIZE)).astype(jnp.int32)
    peak_offsets = with_ends(jax.random.randint(seeds[2], (SECTIONS, PATCHES, 2), -12, 13), jax.random.fold_in(seeds[2], 1), -12, 12).astype(jnp.int32)
    node_valid = with_ends((jax.random.randint(seeds[3], (SECTIONS, PATCHES), 0, 4) < 3).astype(jnp.int32), jax.random.fold_in(seeds[3], 1), 0, 1)
    return dict(features=features, intersection=intersection, peak_offsets=peak_offsets, node_valid=node_valid)


KAPPA = 1.0
STEP_SIZE = 0.2
UNIT_SCALE = 0.125

def dft_tables(width):
    counter = jnp.arange(width, dtype=jnp.int32)
    phases = counter[:, None] * counter[None, :] % width
    angles = 2.0 * math.pi / width * phases.astype(jnp.float32)
    return (jnp.cos(angles), jnp.sin(angles))

def spectrum(patches, cosine_table, sine_table):
    width = cosine_table.shape[0]
    highest = lax.Precision.HIGHEST
    joined = jnp.concatenate([cosine_table, -sine_table], axis=1).astype(jnp.float32)
    halves = jnp.einsum('pcxy,yl->pcxl', patches.astype(jnp.float32), joined, precision=highest).astype(jnp.bfloat16)
    half_re = halves[..., :width].astype(jnp.float32)
    half_im = halves[..., width:].astype(jnp.float32)
    cosine32 = cosine_table.astype(jnp.float32)
    sine32 = sine_table.astype(jnp.float32)
    real_part = jnp.einsum('kx,pcxl->pckl', cosine32, half_re, precision=highest) + jnp.einsum('kx,pcxl->pckl', sine32, half_im, precision=highest)
    imag_part = jnp.einsum('kx,pcxl->pckl', cosine32, half_im, precision=highest) - jnp.einsum('kx,pcxl->pckl', sine32, half_re, precision=highest)
    return (real_part.astype(jnp.bfloat16), imag_part.astype(jnp.bfloat16))

def correlate(own_re, own_im, near_re, near_im, peaks_now):
    width = own_re.shape[-1]
    channels = own_re.shape[1]
    own_re32 = own_re.astype(jnp.float32)
    own_im32 = own_im.astype(jnp.float32)
    near_re32 = near_re.astype(jnp.float32)
    near_im32 = near_im.astype(jnp.float32)
    cross_re = lax.optimization_barrier(jnp.sum(own_re32 * near_re32 + own_im32 * near_im32, axis=1))
    cross_im = lax.optimization_barrier(jnp.sum(own_re32 * near_im32 - own_im32 * near_re32, axis=1))
    damping = jnp.sqrt(cross_re * cross_re + cross_im * cross_im) + width * width * math.sqrt(channels)
    white_re = cross_re / damping
    white_im = cross_im / damping
    row_steps = jnp.array([0, -1, 1, 0, 0], dtype=jnp.int32)
    col_steps = jnp.array([0, 0, 0, -1, 1], dtype=jnp.int32)
    rows = (peaks_now[:, 0:1] + row_steps[None, :]) % width
    cols = (peaks_now[:, 1:2] + col_steps[None, :]) % width
    counter = jnp.arange(width, dtype=jnp.int32)
    row_angle = 2.0 * math.pi / width * (rows[:, :, None] * counter[None, None, :] % width).astype(jnp.float32)
    col_angle = 2.0 * math.pi / width * (cols[:, :, None] * counter[None, None, :] % width).astype(jnp.float32)
    row_cos = jnp.cos(row_angle)
    row_sin = jnp.sin(row_angle)
    col_cos = jnp.cos(col_angle)
    col_sin = jnp.sin(col_angle)
    highest = lax.Precision.HIGHEST
    total = jnp.einsum('pek,pkl,pel->pe', row_cos, white_re, col_cos, precision=highest) - jnp.einsum('pek,pkl,pel->pe', row_sin, white_re, col_sin, precision=highest) - jnp.einsum('pek,pkl,pel->pe', row_cos, white_im, col_sin, precision=highest) - jnp.einsum('pek,pkl,pel->pe', row_sin, white_im, col_cos, precision=highest)
    return total * (2.0 / width)

def refine(scores_now, peaks_now, valid_now):
    centre = scores_now[:, 0]
    spread_row = jnp.abs(scores_now[:, 1]) + jnp.abs(centre) + jnp.abs(scores_now[:, 2]) + 1.0
    spread_col = jnp.abs(scores_now[:, 3]) + jnp.abs(centre) + jnp.abs(scores_now[:, 4]) + 1.0
    sub_row = 0.5 * (scores_now[:, 2] - scores_now[:, 1]) / spread_row
    sub_col = 0.5 * (scores_now[:, 4] - scores_now[:, 3]) / spread_col
    offsets = UNIT_SCALE * (peaks_now.astype(jnp.float32) + jnp.stack([sub_row, sub_col], axis=-1))
    weights = valid_now.astype(jnp.float32) * (1.0 + jnp.tanh(centre))
    return (offsets, weights)

def reference(features, intersection, peak_offsets, node_valid):
    cosine_full, sine_full = dft_tables(W)
    cosine_table = cosine_full.astype(jnp.bfloat16)
    sine_table = sine_full.astype(jnp.bfloat16)
    sources = (jnp.arange(STRIPS, dtype=jnp.int32)[None, :, None] * P_SIZE + intersection).reshape(SECTIONS, PATCHES).astype(jnp.int32)
    not_first = (jnp.arange(SECTIONS) > 0).astype(jnp.float32)

    def per_section(carry, inputs):
        before_re, before_im = carry
        patches, source, peaks_now, valid_now, flag = inputs
        own_re, own_im = spectrum(patches, cosine_table, sine_table)
        near_re = jnp.take(before_re, source, axis=0)
        near_im = jnp.take(before_im, source, axis=0)
        scores_now = correlate(own_re, own_im, near_re, near_im, peaks_now)
        offsets, weights = refine(scores_now, peaks_now, valid_now)
        return ((own_re, own_im), (scores_now, offsets, weights * flag))
    blank = jnp.zeros((PATCHES, C, W, W), jnp.bfloat16)
    unused, outputs = lax.scan(per_section, (blank, blank), (features, sources, peak_offsets, node_valid, not_first))
    scores, offsets, weights = outputs
    numer = lax.optimization_barrier(jnp.sum(weights[:, :, None] * offsets, axis=1))
    denom = lax.optimization_barrier(jnp.sum(weights, axis=1)) + 1.0
    drift = numer / denom[:, None]
    running = jnp.cumsum(drift, axis=0)
    positions = jnp.broadcast_to(running[:, None, :], (SECTIONS, PATCHES, 2)).astype(jnp.float32)
    zero_row = jnp.zeros((1, PATCHES, 2), jnp.float32)
    zero_col = jnp.zeros((SECTIONS, 1, 2), jnp.float32)
    weight_next = jnp.concatenate([weights[1:], jnp.zeros((1, PATCHES), jnp.float32)], axis=0)
    offset_next = jnp.concatenate([offsets[1:], zero_row], axis=0)
    for iteration in range(ITERS):
        prev_rows = jnp.concatenate([zero_row, positions[:-1]], axis=0)
        next_rows = jnp.concatenate([positions[1:], zero_row], axis=0)
        below = weights[:, :, None] * (positions - prev_rows - offsets)
        above = weight_next[:, :, None] * (next_rows - positions - offset_next)
        link_left = jnp.concatenate([zero_col, positions[:, 1:] - positions[:, :-1]], axis=1)
        link_right = jnp.concatenate([positions[:, :-1] - positions[:, 1:], zero_col], axis=1)
        force = below - above + KAPPA * (link_left + link_right)
        positions = positions - STEP_SIZE * force
    return (scores, positions)
```

```python
import functools
import math

import jax
import jax.numpy as jnp
import ml_dtypes
import numpy as np
from jax import lax
from jax.experimental import pallas as pl
from jax.experimental.pallas import tpu as pltpu
from jax.sharding import PartitionSpec as P

ITERS = 8
KAPPA = 1.0
STEP_SIZE = 0.2
UNIT_SCALE = 0.125

WIDTH = 160
HALF = 80
LANES = 128
BATCH = 8
GROUPS = 5
PACKED = GROUPS * LANES
CHANNELS = 32
CHUNKS = 2
VMEM_LIMIT = 56 * 1024 * 1024

SHIFTS = [(HALF * i) % LANES for i in range(BATCH)]


def tables():
    counter = np.arange(WIDTH)
    angles = 2.0 * math.pi / WIDTH * (counter[:, None] * counter[None, :] % WIDTH)
    cosine = np.cos(angles)
    sine = np.sin(angles)
    cos_part = cosine[:HALF]
    sin_part = np.concatenate([cosine[HALF : HALF + 1], sine[1:HALF]], axis=0)
    rows = np.concatenate([cos_part, sin_part], axis=0)
    columns = np.zeros((BATCH, WIDTH, 2 * LANES))
    for i, shift in enumerate(SHIFTS):
        lanes = (np.arange(HALF) + shift) % LANES
        columns[i][:, lanes] = cos_part.T
        columns[i][:, LANES + lanes] = sin_part.T
    return columns.astype(ml_dtypes.bfloat16), rows.astype(ml_dtypes.bfloat16)


def dft_kernel(place_ref, image_ref, columns_ref, rows_ref, out_ref):
    lane = lax.broadcasted_iota(jnp.int32, (16, LANES), 1)
    row = lax.broadcasted_iota(jnp.int32, (16, LANES), 0)
    parts = {}

    def spectrum(i):
        half = jnp.dot(
            image_ref[0, 0, i], columns_ref[i], preferred_element_type=jnp.float32
        ).astype(jnp.bfloat16)
        whole = jnp.dot(rows_ref[...], half, preferred_element_type=jnp.float32)
        cc, cs = whole[:HALF, :LANES], whole[:HALF, LANES:]
        sc, ss = whole[HALF:, :LANES], whole[HALF:, LANES:]
        first = lane[:1] == SHIFTS[i]
        zero = jnp.zeros_like(cc)
        ss0 = jnp.where(first, zero, ss)
        cs0 = jnp.where(first, zero, cs)
        re_low = cc - ss0
        im_low = -(cs0 + sc)
        re_high = jnp.where(first, cs, cc + ss0)
        im_high = jnp.where(first, ss, sc - cs0)
        edge = row == 0
        start = lambda x: x[:16]
        e_cc, e_cs, e_sc, e_ss = start(cc), start(cs), start(sc), start(ss)
        corner = lane == SHIFTS[i]

        def fixed(whole_part, edge_value):
            return jnp.concatenate(
                [jnp.where(edge, edge_value, whole_part[:16]), whole_part[16:]], axis=0
            )

        return (
            (fixed(re_low, e_cc), fixed(re_high, jnp.where(corner, e_cs, e_sc))),
            (
                fixed(im_low, jnp.where(corner, -e_sc, -e_cs)),
                fixed(im_high, jnp.where(corner, e_ss, -e_ss)),
            ),
        )

    def put(group, pieces):
        low = lane[:1]
        for c in range(2):
            for h in range(2):
                value = parts[pieces[-1][1]][c][h]
                for end, image in pieces[-2::-1]:
                    value = jnp.where(low < end, parts[image][c][h], value)
                out_ref[0, c, h * HALF : (h + 1) * HALF, group * LANES : (group + 1) * LANES] = (
                    value.astype(jnp.bfloat16)
                )

    parts[0] = spectrum(0)
    parts[1] = spectrum(1)
    put(0, [(80, 0), (128, 1)])
    parts[2] = spectrum(2)
    parts[3] = spectrum(3)
    put(1, [(32, 1), (112, 2), (128, 3)])
    parts[4] = spectrum(4)
    put(2, [(64, 3), (128, 4)])
    parts[5] = spectrum(5)
    parts[6] = spectrum(6)
    put(3, [(16, 4), (96, 5), (128, 6)])
    parts[7] = spectrum(7)
    put(4, [(48, 6), (128, 7)])


def spectra(features, place, columns, rows, count):
    return pl.pallas_call(
        dft_kernel,
        grid_spec=pltpu.PrefetchScalarGridSpec(
            num_scalar_prefetch=1,
            grid=(count,),
            in_specs=[
                pl.BlockSpec(
                    (1, 1, BATCH, WIDTH, WIDTH),
                    lambda n, place: (place[3 * n], place[3 * n + 1], place[3 * n + 2], 0, 0),
                ),
                pl.BlockSpec((BATCH, WIDTH, 2 * LANES), lambda n, place: (0, 0, 0)),
                pl.BlockSpec((WIDTH, WIDTH), lambda n, place: (0, 0)),
            ],
            out_specs=pl.BlockSpec((1, 2, WIDTH, PACKED), lambda n, place: (n, 0, 0, 0)),
        ),
        out_shape=jax.ShapeDtypeStruct((count, 2, WIDTH, PACKED), jnp.bfloat16),
        compiler_params=pltpu.CompilerParams(vmem_limit_bytes=VMEM_LIMIT),
        cost_estimate=pl.CostEstimate(
            flops=count * BATCH * 2 * 2 * WIDTH * 256 * 256,
            bytes_accessed=count * BATCH * 140000,
            transcendentals=0,
        ),
    )(place, features, columns, rows)


def cross_rows(own_refs, near_refs, at, start):
    lane = lax.broadcasted_iota(jnp.int32, (16, LANES), 1)
    sums = []
    for group in range(GROUPS):
        lanes = slice(group * LANES, (group + 1) * LANES)
        real = imag = both = None
        for own, near in zip(own_refs, near_refs):
            for n in range(own[1], own[2]):
                m = n - own[1] + near[1]
                own_re = own[0][own[3] + (n, 0, pl.ds(start, 16), lanes)].astype(jnp.float32)
                own_im = own[0][own[3] + (n, 1, pl.ds(start, 16), lanes)].astype(jnp.float32)
                near_re = near[0][near[3] + (m, 0, pl.ds(start, 16), lanes)].astype(jnp.float32)
                near_im = near[0][near[3] + (m, 1, pl.ds(start, 16), lanes)].astype(jnp.float32)
                ii = own_im * near_im
                re = own_re * near_re + ii
                im = own_re * near_im - own_im * near_re
                real = re if real is None else real + re
                imag = im if imag is None else imag + im
                both = ii if both is None else both + ii
        sums.append((real, imag, both))
    totals = []
    for c in range(3):
        g = [s[c] for s in sums]
        windows = [
            (0, g[0]),
            (80, jnp.where(lane >= 80, g[0], g[1])),
            (32, g[1]),
            (112, jnp.where(lane >= 112, g[1], g[2])),
            (64, jnp.where(lane >= 64, g[2], g[3])),
            (16, g[3]),
            (96, jnp.where(lane >= 96, g[3], g[4])),
            (48, g[4]),
        ]
        total = None
        for shift, value in windows:
            moved = value if shift == 0 else pltpu.roll(value, LANES - shift, 1)
            total = moved if total is None else total + moved
        totals.append(total)
    return totals


def cross_into(sum_ref, own_refs, near_refs, sign, before_ref=None, at=None):
    def step(n, carry):
        start = pl.multiple_of(n * 16, 16)
        real, imag, both = cross_rows(own_refs, near_refs, at, start)
        values = [real, sign * imag, both]
        for c in range(3):
            value = values[c]
            if before_ref is not None:
                value = value + before_ref[at, c, pl.ds(start, 16), :]
            sum_ref[c, pl.ds(start, 16), :] = value
        return carry

    lax.fori_loop(0, WIDTH // 16, step, 0)


def scores_of(sum_ref, row_phase_ref, col_phase_ref, node):
    lane = lax.broadcasted_iota(jnp.int32, (1, LANES), 1)
    damp = WIDTH * WIDTH * math.sqrt(CHANNELS)
    halves = []
    extra = []
    for h in range(2):
        rows = slice(h * HALF, (h + 1) * HALF)
        real, imag = sum_ref[0, rows, :], sum_ref[1, rows, :]
        both = sum_ref[2, h * HALF : h * HALF + 8, :]
        row = lax.broadcasted_iota(jnp.int32, (HALF, LANES), 0)
        corner = (row == 0) & (lax.broadcasted_iota(jnp.int32, (HALF, LANES), 1) == 0)
        size = jnp.sqrt(real * real + imag * imag) + damp
        white_re, white_im = real / size, imag / size
        ii = both[0:1, :]
        rr = real[0:1, :] - ii
        z_rr = 0.5 * rr / (jnp.abs(rr) + damp)
        z_ii = 0.5 * ii / (jnp.abs(ii) + damp)
        stays, goes = (z_rr, z_ii) if h == 0 else (z_ii, z_rr)
        white_re = jnp.where(corner, jnp.broadcast_to(stays, (HALF, LANES)), white_re)
        white_im = jnp.where(corner, 0.0, white_im)
        halves.append((white_re, white_im))
        extra.append(jnp.where(lane == 0, goes, 0.0))
    sums = []
    for a in range(3):
        pair = []
        for h in range(2):
            rows = slice(h * HALF, (h + 1) * HALF)
            cos = row_phase_ref[node, rows, a : a + 1]
            sin = row_phase_ref[node, rows, 3 + a : 4 + a]
            white_re, white_im = halves[h]
            y_re = jnp.sum(white_re * cos - white_im * sin, axis=0, keepdims=True)
            y_im = jnp.sum(white_re * sin + white_im * cos, axis=0, keepdims=True)
            if h == 0:
                y_re = y_re + extra[0] * row_phase_ref[node, HALF : HALF + 1, a : a + 1]
            else:
                y_re = y_re + extra[1]
            pair.append((y_re, y_im))
        sums.append(pair)
    out = []
    for a, b in ((0, 0), (1, 0), (2, 0), (0, 1), (0, 2)):
        total = None
        for h in range(2):
            cos = col_phase_ref[node, 4 * b + 2 * h : 4 * b + 2 * h + 1, :]
            sin = col_phase_ref[node, 4 * b + 2 * h + 1 : 4 * b + 2 * h + 2, :]
            term = sums[a][h][0] * cos - sums[a][h][1] * sin
            total = term if total is None else total + term
        out.append(jnp.sum(total, axis=1, keepdims=True) * (4.0 / WIDTH))
    return out


def node_row(z, node_ref, node):
    lane = lax.broadcasted_iota(jnp.int32, (1, LANES), 1)
    wide = [jnp.broadcast_to(value, (1, LANES)) for value in z]
    spread_row = jnp.abs(wide[1]) + jnp.abs(wide[0]) + jnp.abs(wide[2]) + 1.0
    spread_col = jnp.abs(wide[3]) + jnp.abs(wide[0]) + jnp.abs(wide[4]) + 1.0
    peak_row = node_ref[node, 0].astype(jnp.float32)
    peak_col = node_ref[node, 1].astype(jnp.float32)
    valid = node_ref[node, 2].astype(jnp.float32)
    off_row = UNIT_SCALE * (peak_row + 0.5 * (wide[2] - wide[1]) / spread_row)
    off_col = UNIT_SCALE * (peak_col + 0.5 * (wide[4] - wide[3]) / spread_col)
    weight = valid * (1.0 + jnp.tanh(wide[0]))
    row = jnp.zeros((1, LANES), jnp.float32)
    for n, value in enumerate([weight, off_row, off_col] + wide):
        row = jnp.where(lane == n, value, row)
    return row


def local_kernel(
    flag_ref, node_ref, up0_ref, up1_ref, down0_ref, down1_ref, rest_ref, row_ref, col_ref, out_ref,
    sum_ref,
):
    per = CHANNELS // BATCH // CHUNKS
    up = [(up0_ref, 0, per, ()), (up1_ref, 0, per, ())]
    down = [(down0_ref, 0, per, ()), (down1_ref, 0, per, ())]
    first = [(rest_ref, 0, per, ()), (rest_ref, per, 2 * per, ())]
    second = [(rest_ref, 2 * per, 3 * per, ()), (rest_ref, 3 * per, 4 * per, ())]
    same = flag_ref[0] == 1
    lane = lax.broadcasted_iota(jnp.int32, (1, LANES), 1)

    @pl.when(same)
    def _():
        cross_into(sum_ref.at[0], up, down, 1.0)
        cross_into(sum_ref.at[1], second, first, 1.0)

    @pl.when(jnp.logical_not(same))
    def _():
        cross_into(sum_ref.at[0], up, first, 1.0)
        cross_into(sum_ref.at[1], second, down, 1.0)

    total = jnp.zeros((1, LANES), jnp.float32)
    for n in range(2):
        row = node_row(scores_of(sum_ref.at[n], row_ref, col_ref, 1 + n), node_ref, 1 + n)
        total = total + pltpu.roll(row, 16 + 8 * n, 1)
    out_ref[...] = total


def first_kernel(rest_ref, above_ref, below_ref, out_ref):
    per = CHANNELS // BATCH // CHUNKS
    for n, ref in ((0, below_ref), (1, above_ref)):
        mine = [(rest_ref, n * 2 * per, n * 2 * per + per, ())]
        theirs = [(ref, 0, per, ())]
        cross_into(out_ref.at[n], mine, theirs, 1.0 if n == 0 else -1.0)


def last_kernel(
    flag_ref, node_ref, rest_ref, above_ref, below_ref, before_ref, row_ref, col_ref, local_ref,
    out_ref, sum_ref,
):
    per = CHANNELS // BATCH // CHUNKS
    total = local_ref[...]
    for n, ref in ((0, below_ref), (1, above_ref)):
        mine = [(rest_ref, n * 2 * per + per, n * 2 * per + 2 * per, ())]
        theirs = [(ref, 0, per, ())]
        cross_into(sum_ref.at[n], mine, theirs, 1.0 if n == 0 else -1.0, before_ref, n)
    lane = lax.broadcasted_iota(jnp.int32, (1, LANES), 1)
    for n in range(2):
        node = 3 * n
        row = node_row(scores_of(sum_ref.at[n], row_ref, col_ref, node), node_ref, node)
        slot = node_ref[node, 3]
        low = pltpu.roll(row, 32 * n, 1) if n else row
        high = pltpu.roll(row, 32 * n + 8, 1)
        total = total + jnp.where(slot == 0, low, high)
    out_ref[...] = jnp.broadcast_to(total[None], out_ref.shape)


def relax_kernel(place_ref, all_ref, scores_ref, positions_ref, hold_ref, *, devices):
    sec, strip = place_ref[0], place_ref[1]
    strips = 4
    lane = lax.broadcasted_iota(jnp.int32, (8, LANES), 1)
    row = lax.broadcasted_iota(jnp.int32, (8, LANES), 0)
    seat = lane % 64
    slots = []
    for t in range(strips):
        block = all_ref[t * 64 : (t + 1) * 64, :]
        turned = jnp.concatenate([block, jnp.zeros((64, LANES), jnp.float32)], axis=0).T
        slots.append([turned[8 * n : 8 * n + 8] for n in range(6)])
    firsts, seconds = [], []
    for t in range(strips):
        for i in range(2):
            ahead = jnp.where(lane == 0, 0.0, pltpu.roll(slots[t][4 + i], 1, 1))
            firsts.append(slots[t][i] + ahead)
            seconds.append(slots[t][2 + i])

    def field(arrays, comp):
        return jnp.concatenate([a[comp : comp + 1] for a in arrays], axis=0)

    def both(low, high):
        return jnp.where(lane < 64, low, pltpu.roll(high, 64, 1))

    w_a = field(firsts, 0)
    w_a = jnp.where(lane == 0, 0.0, w_a)
    w_b = field(seconds, 0)
    w_a, w_b = both(w_a, w_a), both(w_b, w_b)
    o_a = both(field(firsts, 1), field(firsts, 2))
    o_b = both(field(seconds, 1), field(seconds, 2))
    drift_a = jnp.sum(w_a * o_a, axis=0, keepdims=True) / (
        jnp.sum(w_a, axis=0, keepdims=True) + 1.0
    )
    drift_b = jnp.sum(w_b * o_b, axis=0, keepdims=True) / (
        jnp.sum(w_b, axis=0, keepdims=True) + 1.0
    )
    drift_a = jnp.broadcast_to(drift_a, (8, LANES))
    drift_b = jnp.broadcast_to(drift_b, (8, LANES))
    run = drift_a + drift_b
    for shift in (1, 2, 4, 8, 16, 32):
        run = run + jnp.where(seat >= shift, pltpu.roll(run, shift, 1), 0.0)
    p_b = run
    p_a = run - drift_b

    def links(p):
        left = jnp.where(row > 0, pltpu.roll(p, 1, 0), p)
        right = jnp.where(row < 7, pltpu.roll(p, 7, 0), p)
        return (p - left) + (p - right)

    for _ in range(ITERS):
        e_a = w_a * (p_a - pltpu.roll(p_b, 1, 1) - o_a)
        e_b = w_b * (p_b - p_a - o_b)
        e_next = pltpu.roll(e_a, LANES - 1, 1)
        n_a = p_a - STEP_SIZE * (e_a - e_b + KAPPA * links(p_a))
        n_b = p_b - STEP_SIZE * (e_b - e_next + KAPPA * links(p_b))
        p_a, p_b = n_a, n_b
    for s, p in enumerate((p_a, p_b)):
        first = jnp.sum(jnp.where(lane == sec, p, 0.0), axis=1, keepdims=True)
        other = jnp.sum(jnp.where(lane == sec + 64, p, 0.0), axis=1, keepdims=True)
        hold_ref[...] = jnp.where(lane == 0, first, other)
        for i in range(2):
            positions_ref[s, i : i + 1, :] = hold_ref[pl.ds(2 * strip + i, 1), :][:, :2]
    own = all_ref[pl.ds(strip * 64 + sec, 1), :]
    earlier = all_ref[pl.ds(strip * 64 + jnp.maximum(sec - 1, 0), 1), :]
    earlier = jnp.where(sec > 0, earlier, 0.0)
    for i in range(2):
        value = pltpu.roll(own, LANES - (8 * i + 3), 1) + pltpu.roll(
            earlier, LANES - (32 + 8 * i + 3), 1
        )
        scores_ref[0, i : i + 1, :] = value[:, :5]
        scores_ref[1, i : i + 1, :] = pltpu.roll(own, LANES - (16 + 8 * i + 3), 1)[:, :5]


def phases(peaks):
    steps = jnp.array([0, -1, 1], jnp.int32)
    rows = np.concatenate([np.arange(HALF), [HALF], -np.arange(1, HALF)]).astype(np.int32)
    u = peaks[:, 0:1] + steps[None, :]
    v = peaks[:, 1:2] + steps[None, :]
    unit = 2.0 * math.pi / WIDTH
    row_angle = unit * jnp.mod(rows[None, :, None] * u[:, None, :], WIDTH).astype(jnp.float32)
    row_phase = jnp.concatenate(
        [jnp.cos(row_angle), jnp.sin(row_angle), jnp.zeros(row_angle.shape[:2] + (2,))], axis=-1
    )
    low = np.zeros(LANES, np.int32)
    low[:HALF] = np.arange(HALF)
    high = low.copy()
    high[0] = HALF
    used = (np.arange(LANES) < HALF).astype(np.float32)
    freq = np.stack([low, high])
    col_angle = unit * jnp.mod(freq[None, None] * v[:, :, None, None], WIDTH).astype(jnp.float32)
    col_phase = jnp.stack([jnp.cos(col_angle), jnp.sin(col_angle)], axis=3) * used
    col_phase = col_phase.reshape(peaks.shape[0], 12, LANES)
    col_phase = jnp.concatenate([col_phase, jnp.zeros((peaks.shape[0], 4, LANES))], axis=1)
    return row_phase.astype(jnp.float32), col_phase.astype(jnp.float32)


def body(features, intersection, peak_offsets, node_valid):
    secs, strips = lax.axis_size("sec"), lax.axis_size("strip")
    sec, strip = lax.axis_index("sec"), lax.axis_index("strip")
    columns, rows = tables()
    columns, rows = jnp.asarray(columns), jnp.asarray(rows)
    up = [(i, i + 1) for i in range(secs - 1)]
    down = [(i + 1, i) for i in range(secs - 1)]
    batches = CHANNELS // BATCH
    per = batches // CHUNKS

    keep = intersection[0, 0, 0]
    give = 1 - keep
    flag = (intersection[1, 0, 0] == give).astype(jnp.int32).reshape(1)

    def take(values, n):
        return jnp.where(n == 0, values[0], values[1])

    ahead = lax.ppermute(
        jnp.concatenate(
            [
                take(peak_offsets[0], give),
                take(node_valid[0], give).reshape(1),
                give.reshape(1),
            ]
        ),
        "sec",
        down,
    )
    one = lambda a: a.reshape(1).astype(jnp.int32)
    zero = jnp.zeros((1,), jnp.int32)
    nodes = jnp.stack(
        [
            jnp.concatenate([take(peak_offsets[0], keep), one(take(node_valid[0], keep)), one(keep)]),
            jnp.concatenate([peak_offsets[1, 0], one(node_valid[1, 0]), zero]),
            jnp.concatenate([peak_offsets[1, 1], one(node_valid[1, 1]), zero]),
            ahead,
        ]
    )
    row_phase, col_phase = phases(nodes[:, :2])

    ups, downs, aboves, belows = [], [], [], []
    for chunk in range(CHUNKS):
        place = np.array([[1, 0, chunk * per + n] for n in range(per)], np.int32).reshape(-1)
        ups.append(spectra(features, jnp.asarray(place), columns, rows, per))
        belows.append(lax.ppermute(ups[-1], "sec", up))
        place = jnp.stack(
            [p for n in range(per) for p in (jnp.int32(0), give, jnp.int32(chunk * per + n))]
        )
        downs.append(spectra(features, place, columns, rows, per))
        aboves.append(lax.ppermute(downs[-1], "sec", down))
    place = jnp.stack(
        [
            p
            for section, patch in ((0, keep), (1, jnp.int32(1)))
            for n in range(batches)
            for p in (jnp.int32(section), patch, jnp.int32(n))
        ]
    )
    rest = spectra(features, place, columns, rows, 2 * batches)

    smem = pl.BlockSpec(memory_space=pltpu.SMEM)
    vmem = pl.BlockSpec(memory_space=pltpu.VMEM)
    params = pltpu.CompilerParams(vmem_limit_bytes=VMEM_LIMIT)
    sums = pltpu.VMEM((2, 3, WIDTH, LANES), jnp.float32)
    local = pl.pallas_call(
        local_kernel,
        in_specs=[smem, smem] + [vmem] * 7,
        out_specs=vmem,
        out_shape=jax.ShapeDtypeStruct((1, LANES), jnp.float32),
        scratch_shapes=[sums],
        compiler_params=params,
        cost_estimate=pl.CostEstimate(
            flops=64 * 25600 * 200, bytes_accessed=7000000, transcendentals=0
        ),
    )(flag, nodes, ups[0], ups[1], downs[0], downs[1], rest, row_phase, col_phase)
    partial = pl.pallas_call(
        first_kernel,
        in_specs=[vmem] * 3,
        out_specs=vmem,
        out_shape=jax.ShapeDtypeStruct((2, 3, WIDTH, LANES), jnp.float32),
        compiler_params=params,
        cost_estimate=pl.CostEstimate(
            flops=32 * 25600 * 200, bytes_accessed=4000000, transcendentals=0
        ),
    )(rest, aboves[0], belows[0])
    total = secs * strips
    message = pl.pallas_call(
        last_kernel,
        in_specs=[smem, smem] + [vmem] * 7,
        out_specs=vmem,
        out_shape=jax.ShapeDtypeStruct((total, 1, LANES), jnp.float32),
        scratch_shapes=[sums],
        compiler_params=params,
        cost_estimate=pl.CostEstimate(
            flops=32 * 25600 * 200, bytes_accessed=4000000, transcendentals=0
        ),
    )(flag, nodes, rest, aboves[1], belows[1], partial, row_phase, col_phase, local)

    gathered = lax.all_to_all(message, ("strip", "sec"), 0, 0).reshape(strips, secs, LANES)
    if secs < 64:
        gathered = jnp.pad(gathered, ((0, 0), (0, 64 - secs), (0, 0)))
    gathered = gathered.reshape(strips * 64, LANES)
    scores, positions = pl.pallas_call(
        functools.partial(relax_kernel, devices=secs),
        in_specs=[smem, vmem],
        out_specs=[vmem, vmem],
        out_shape=[
            jax.ShapeDtypeStruct((2, 2, 5), jnp.float32),
            jax.ShapeDtypeStruct((2, 2, 2), jnp.float32),
        ],
        scratch_shapes=[pltpu.VMEM((8, LANES), jnp.float32)],
        compiler_params=params,
    )(jnp.stack([sec, strip]).astype(jnp.int32), gathered)
    return scores, positions


def solution(mesh):
    placed = (
        P("sec", "strip", None, None, None),
        P("sec", "strip", None),
        P("sec", "strip", None),
        P("sec", "strip"),
    )
    return jax.shard_map(
        body,
        mesh=mesh,
        in_specs=placed,
        out_specs=(P("sec", "strip", None), P("sec", "strip", None)),
        check_vma=False,
    )
```

```python
import functools
import math

import jax
import jax.numpy as jnp
import ml_dtypes
import numpy as np
from jax import lax
from jax.experimental import pallas as pl
from jax.experimental.pallas import tpu as pltpu
from jax.sharding import PartitionSpec as P

ITERS = 8
KAPPA = 1.0
STEP_SIZE = 0.2
UNIT_SCALE = 0.125

WIDTH = 160
HALF = 80
LANES = 128
BATCH = 8
GROUPS = 5
PACKED = GROUPS * LANES
CHANNELS = 32
BATCHES = CHANNELS // BATCH
REACH = 13
BLOCK = 2 * WIDTH
NOTE = 16

SHIFTS = [(HALF * i) % LANES for i in range(BATCH)]
PIECES = [
    [(80, 0), (128, 1)],
    [(32, 1), (112, 2), (128, 3)],
    [(64, 3), (128, 4)],
    [(16, 4), (96, 5), (128, 6)],
    [(48, 6), (128, 7)],
]
STARTS = [[0, 80], [32, 112], [64], [16, 96], [48]]
ROW_FREQ = np.concatenate([np.arange(HALF), [HALF], -np.arange(1, HALF)])


def angle(product):
    return 2.0 * math.pi / WIDTH * (product % WIDTH)


def tables():
    counter = np.arange(WIDTH)
    angles = angle(counter[:, None] * counter[None, :])
    cosine, sine = np.cos(angles), np.sin(angles)
    cos_part = cosine[:HALF]
    sin_part = np.concatenate([cosine[HALF : HALF + 1], sine[1:HALF]], axis=0)
    rows = np.concatenate([cos_part, sin_part], axis=0)
    columns = np.zeros((BATCH, WIDTH, 2 * LANES))
    for i, shift in enumerate(SHIFTS):
        lanes = (np.arange(HALF) + shift) % LANES
        columns[i][:, lanes] = cos_part.T
        columns[i][:, LANES + lanes] = sin_part.T
    return columns.astype(ml_dtypes.bfloat16), rows.astype(ml_dtypes.bfloat16)


def phase_tables():
    peaks = np.arange(-REACH, REACH + 1)
    rows = np.zeros((WIDTH, LANES))
    a = angle(ROW_FREQ[:, None] * peaks[None, :])
    rows[:, : len(peaks)] = np.cos(a)
    rows[:, 64 : 64 + len(peaks)] = np.sin(a)
    unit = np.zeros((2, WIDTH, LANES))
    unit[0] = np.cos(angle(ROW_FREQ))[:, None]
    unit[1] = np.sin(angle(ROW_FREQ))[:, None]
    columns = np.zeros((4, 32, LANES))
    low = np.arange(HALF)
    high = low.copy()
    high[0] = HALF
    for h, freq in enumerate((low, high)):
        b = angle(peaks[:, None] * freq[None, :])
        columns[2 * h, : len(peaks), :HALF] = np.cos(b)
        columns[2 * h + 1, : len(peaks), :HALF] = np.sin(b)
    return rows.astype(np.float32), unit.astype(np.float32), columns.astype(np.float32)


def transform(image, columns_ref, rows_ref, packed_ref, store):
    lane2 = lax.broadcasted_iota(jnp.int32, (1, 2 * LANES), 1) % LANES
    halves = {}

    def half(i):
        halves[i] = jnp.dot(image(i), columns_ref[i], preferred_element_type=jnp.float32)

    def pack(group):
        pieces = PIECES[group]
        value = halves[pieces[-1][1]]
        for end, i in pieces[-2::-1]:
            value = jnp.where(lane2 < end, halves[i], value)
        packed_ref[:, group * 2 * LANES : (group + 1) * 2 * LANES] = value.astype(jnp.bfloat16)

    lane = lax.broadcasted_iota(jnp.int32, (1, LANES), 1)
    edge = lax.broadcasted_iota(jnp.int32, (16, LANES), 0) == 0

    def finish(group):
        whole = jnp.dot(
            rows_ref[...],
            packed_ref[:, group * 2 * LANES : (group + 1) * 2 * LANES],
            preferred_element_type=jnp.float32,
        )
        first = lane == STARTS[group][0]
        for start in STARTS[group][1:]:
            first = first | (lane == start)
        cc, cs = whole[:HALF, :LANES], whole[:HALF, LANES:]
        sc, ss = whole[HALF:, :LANES], whole[HALF:, LANES:]
        ss0 = jnp.where(first, 0.0, ss)
        cs0 = jnp.where(first, 0.0, cs)
        values = [
            (0, 0, cc - ss0, cc),
            (0, 1, jnp.where(first, cs, cc + ss0), jnp.where(first, cs, sc)),
            (1, 0, -(cs0 + sc), jnp.where(first, -sc, -cs)),
            (1, 1, jnp.where(first, ss, sc - cs0), jnp.where(first, ss, -ss)),
        ]
        for c, h, value, fixed in values:
            top = jnp.where(edge, fixed[:16], value[:16]).astype(jnp.bfloat16)
            store(c, h * HALF, 16, group, top)
            store(c, h * HALF + 16, HALF - 16, group, value[16:].astype(jnp.bfloat16))

    half(0)
    half(1)
    pack(0)
    half(2)
    half(3)
    pack(1)
    finish(0)
    half(4)
    pack(2)
    finish(1)
    half(5)
    half(6)
    pack(3)
    finish(2)
    half(7)
    pack(4)
    finish(3)
    finish(4)


def plain_kernel(meet_ref, image_ref, columns_ref, rows_ref, out_ref, packed_ref):
    def store(c, row, count, group, value):
        out_ref[c * WIDTH + row : c * WIDTH + row + count, group * LANES : (group + 1) * LANES] = value

    transform(lambda i: image_ref[0, 0, i], columns_ref, rows_ref, packed_ref, store)


def noted_kernel(
    meet_ref, peak_ref, valid_ref, image_ref, columns_ref, rows_ref, out_ref, packed_ref
):
    n = pl.program_id(0)
    base = n * BLOCK

    def store(c, row, count, group, value):
        at = pl.multiple_of(base + c * WIDTH + row, 16)
        out_ref[pl.ds(at, count), group * LANES : (group + 1) * LANES] = value

    transform(lambda i: image_ref[0, 0, i], columns_ref, rows_ref, packed_ref, store)

    @pl.when(n == 0)
    def _():
        give = 1 - meet_ref[0, 0, 0]
        lane = lax.broadcasted_iota(jnp.int32, (NOTE, PACKED), 1)
        note = jnp.zeros((NOTE, PACKED), jnp.float32)
        values = [peak_ref[0, give, 0], peak_ref[0, give, 1], valid_ref[0, give], give]
        for k, value in enumerate(values):
            note = jnp.where(lane == k, value.astype(jnp.float32), note)
        out_ref[BATCHES * BLOCK :, :] = note.astype(jnp.bfloat16)


def dft_cost(count):
    return pl.CostEstimate(
        flops=count * BATCH * 2 * 2 * WIDTH * 256 * 256,
        bytes_accessed=count * BATCH * 140000,
        transcendentals=0,
    )


def spectra(features, meet, columns, rows, where, count):
    return pl.pallas_call(
        plain_kernel,
        grid_spec=pltpu.PrefetchScalarGridSpec(
            num_scalar_prefetch=1,
            grid=(count,),
            in_specs=[
                pl.BlockSpec(
                    (1, 1, BATCH, WIDTH, WIDTH), lambda n, meet: where(n, meet) + (0, 0)
                ),
                pl.BlockSpec((BATCH, WIDTH, 2 * LANES), lambda n, meet: (0, 0, 0)),
                pl.BlockSpec((WIDTH, WIDTH), lambda n, meet: (0, 0)),
            ],
            out_specs=pl.BlockSpec((BLOCK, PACKED), lambda n, meet: (n, 0)),
            scratch_shapes=[pltpu.VMEM((WIDTH, 2 * PACKED), jnp.bfloat16)],
        ),
        out_shape=jax.ShapeDtypeStruct((count * BLOCK, PACKED), jnp.bfloat16),
        compiler_params=pltpu.CompilerParams(
            vmem_limit_bytes=(54 if count == BATCHES else 48) * 1024 * 1024
        ),
        cost_estimate=dft_cost(count),
    )(meet, features, columns, rows)


def noted_spectra(features, meet, peaks, valid, columns, rows):
    shape = (BATCHES * BLOCK + NOTE, PACKED)
    return pl.pallas_call(
        noted_kernel,
        grid_spec=pltpu.PrefetchScalarGridSpec(
            num_scalar_prefetch=3,
            grid=(BATCHES,),
            in_specs=[
                pl.BlockSpec(
                    (1, 1, BATCH, WIDTH, WIDTH),
                    lambda n, meet, peaks, valid: (0, 1 - meet[0, 0, 0], n, 0, 0),
                ),
                pl.BlockSpec((BATCH, WIDTH, 2 * LANES), lambda n, *_: (0, 0, 0)),
                pl.BlockSpec((WIDTH, WIDTH), lambda n, *_: (0, 0)),
            ],
            out_specs=pl.BlockSpec(shape, lambda n, *_: (0, 0)),
            scratch_shapes=[pltpu.VMEM((WIDTH, 2 * PACKED), jnp.bfloat16)],
        ),
        out_shape=jax.ShapeDtypeStruct(shape, jnp.bfloat16),
        compiler_params=pltpu.CompilerParams(vmem_limit_bytes=54 * 1024 * 1024),
        cost_estimate=dft_cost(BATCHES),
    )(meet, peaks, valid, features, columns, rows)


def gather_windows(g):
    lane = lax.broadcasted_iota(jnp.int32, (1, LANES), 1)
    low = lane < 80
    windows = [
        (80, jnp.where(low, g[1], g[0])),
        (32, g[1]),
        (112, jnp.where(lane < 112, g[2], g[1])),
        (64, jnp.where(lane < 64, g[3], g[2])),
        (16, g[3]),
        (96, jnp.where(lane < 96, g[4], g[3])),
        (48, g[4]),
    ]
    total = g[0]
    for shift, value in windows:
        total = total + pltpu.roll(value, LANES - shift, 1)
    return total


def cross_into(sum_ref, edge_ref, own, near, sign):
    def load(side, n, c, start, lanes):
        at = pl.multiple_of(side[1] + n * BLOCK + c * WIDTH + start, 16)
        return side[0][pl.ds(at, 16), lanes].astype(jnp.float32)

    def step(k, carry):
        start = pl.multiple_of(k * 16, 16)
        reals, imags = [], []
        for group in range(GROUPS):
            lanes = slice(group * LANES, (group + 1) * LANES)
            real = imag = None
            for n in range(BATCHES):
                own_re, own_im = (load(own, n, c, start, lanes) for c in range(2))
                near_re, near_im = (load(near, n, c, start, lanes) for c in range(2))
                re = own_re * near_re + own_im * near_im
                im = own_re * near_im - own_im * near_re
                real = re if real is None else real + re
                imag = im if imag is None else imag + im
            reals.append(real)
            imags.append(imag)
        sum_ref[0, pl.ds(start, 16), :] = gather_windows(reals)
        sum_ref[1, pl.ds(start, 16), :] = sign * gather_windows(imags)
        return carry

    lax.fori_loop(0, WIDTH // 16, step, 0)
    for h in range(2):
        boths = []
        for group in range(GROUPS):
            lanes = slice(group * LANES, (group + 1) * LANES)
            both = None
            for n in range(BATCHES):
                ii = load(own, n, 1, h * HALF, lanes) * load(near, n, 1, h * HALF, lanes)
                both = ii if both is None else both + ii
            boths.append(both[:8])
        edge_ref[h] = gather_windows(boths)


def scores_of(sum_ref, edge_ref, row_ref, unit_ref, col_ref, peak_row, peak_col):
    lane = lax.broadcasted_iota(jnp.int32, (1, LANES), 1)
    damp = WIDTH * WIDTH * math.sqrt(CHANNELS)
    sums = {}
    moved = pltpu.roll(row_ref[...], (LANES - REACH) - peak_row, 1)
    for h in range(2):
        rows = slice(h * HALF, (h + 1) * HALF)
        real, imag = sum_ref[0, rows, :], sum_ref[1, rows, :]
        inverse = 1.0 / (jnp.sqrt(real * real + imag * imag) + damp)
        white_re, white_im = real * inverse, imag * inverse
        ii = edge_ref[h][0:1, :]
        rr = real[0:1, :] - ii
        z_rr = 0.5 * rr / (jnp.abs(rr) + damp)
        z_ii = 0.5 * ii / (jnp.abs(ii) + damp)
        stays, goes = (z_rr, z_ii) if h == 0 else (z_ii, z_rr)
        corner = (lax.broadcasted_iota(jnp.int32, (8, LANES), 0) == 0) & (
            lax.broadcasted_iota(jnp.int32, (8, LANES), 1) == 0
        )
        white_re = jnp.concatenate(
            [jnp.where(corner, jnp.broadcast_to(stays, (8, LANES)), white_re[:8]), white_re[8:]], 0
        )
        white_im = jnp.concatenate([jnp.where(corner, 0.0, white_im[:8]), white_im[8:]], 0)
        cos, sin = moved[rows, 0:1], moved[rows, 64:65]
        turned_re = white_re * cos - white_im * sin
        turned_im = white_re * sin + white_im * cos
        unit_cos, unit_sin = unit_ref[0, rows, :], unit_ref[1, rows, :]
        add = lambda x: jnp.sum(x, axis=0, keepdims=True)
        plain_re, plain_im = add(turned_re), add(turned_im)
        cos_re, cos_im = add(turned_re * unit_cos), add(turned_im * unit_cos)
        sin_re, sin_im = add(turned_re * unit_sin), add(turned_im * unit_sin)
        sums[h] = [
            (plain_re, plain_im),
            (cos_re + sin_im, cos_im - sin_re),
            (cos_re - sin_im, cos_im + sin_re),
        ]
        extra = jnp.where(lane == 0, goes, 0.0)
        for a in range(3):
            turn = moved[HALF : HALF + 1, 0:1] * (1.0 if a == 0 else -1.0) if h == 0 else 1.0
            sums[h][a] = (sums[h][a][0] + extra * turn, sums[h][a][1])
    out = []
    for a, b in ((0, 0), (1, 0), (2, 0), (0, -1), (0, 1)):
        total = None
        for h in range(2):
            cos = col_ref[2 * h, pl.ds(peak_col + (REACH + b), 1), :]
            sin = col_ref[2 * h + 1, pl.ds(peak_col + (REACH + b), 1), :]
            term = sums[h][a][0] * cos - sums[h][a][1] * sin
            total = term if total is None else total + term
        out.append(jnp.sum(total, axis=1, keepdims=True) * (4.0 / WIDTH))
    return out


def node_row(z, peak_row, peak_col, valid):
    lane = lax.broadcasted_iota(jnp.int32, (1, LANES), 1)
    wide = [jnp.broadcast_to(value, (1, LANES)) for value in z]
    spread_row = jnp.abs(wide[1]) + jnp.abs(wide[0]) + jnp.abs(wide[2]) + 1.0
    spread_col = jnp.abs(wide[3]) + jnp.abs(wide[0]) + jnp.abs(wide[4]) + 1.0
    off_row = UNIT_SCALE * (
        peak_row.astype(jnp.float32) + 0.5 * (wide[2] - wide[1]) / spread_row
    )
    off_col = UNIT_SCALE * (
        peak_col.astype(jnp.float32) + 0.5 * (wide[4] - wide[3]) / spread_col
    )
    weight = valid.astype(jnp.float32) * (1.0 + jnp.tanh(wide[0]))
    row = jnp.zeros((1, LANES), jnp.float32)
    for n, value in enumerate([weight, off_row, off_col] + wide):
        row = jnp.where(lane == n, value, row)
    return row


def local_kernel(
    meet_ref, peak_ref, valid_ref, up_ref, down_ref, rest_ref, row_ref, unit_ref, col_ref, out_ref,
    sum_ref, edge_ref,
):
    rest = BATCHES * BLOCK
    same = meet_ref[1, 0, 0] == 1 - meet_ref[0, 0, 0]

    @pl.when(same)
    def _():
        cross_into(sum_ref.at[0], edge_ref.at[0], (up_ref, 0), (down_ref, 0), 1.0)
        cross_into(sum_ref.at[1], edge_ref.at[1], (rest_ref, rest), (rest_ref, 0), 1.0)

    @pl.when(jnp.logical_not(same))
    def _():
        cross_into(sum_ref.at[0], edge_ref.at[0], (up_ref, 0), (rest_ref, 0), 1.0)
        cross_into(sum_ref.at[1], edge_ref.at[1], (rest_ref, rest), (down_ref, 0), 1.0)

    total = jnp.zeros((1, LANES), jnp.float32)
    for n in range(2):
        peak = peak_ref[1, n, 0], peak_ref[1, n, 1]
        z = scores_of(sum_ref.at[n], edge_ref.at[n], row_ref, unit_ref, col_ref, *peak)
        total = total + pltpu.roll(node_row(z, *peak, valid_ref[1, n]), 16 + 8 * n, 1)
    out_ref[...] = total


def kept_kernel(
    meet_ref, peak_ref, valid_ref, rest_ref, below_ref, row_ref, unit_ref, col_ref, local_ref,
    out_ref, sum_ref, edge_ref,
):
    keep = meet_ref[0, 0, 0]
    cross_into(sum_ref, edge_ref, (rest_ref, 0), (below_ref, 0), 1.0)
    peak = peak_ref[0, keep, 0], peak_ref[0, keep, 1]
    z = scores_of(sum_ref, edge_ref, row_ref, unit_ref, col_ref, *peak)
    row = node_row(z, *peak, valid_ref[0, keep])
    out_ref[...] = local_ref[...] + jnp.where(keep == 0, row, pltpu.roll(row, 8, 1))


def given_kernel(
    rest_ref, above_ref, row_ref, unit_ref, col_ref, kept_ref, out_ref, sum_ref, edge_ref
):
    cross_into(sum_ref, edge_ref, (rest_ref, BATCHES * BLOCK), (above_ref, 0), -1.0)
    note = above_ref[BATCHES * BLOCK :, :LANES].astype(jnp.float32)[0:1, :]
    lane = lax.broadcasted_iota(jnp.int32, (1, LANES), 1)
    held = [jnp.sum(jnp.where(lane == k, note, 0.0)).astype(jnp.int32) for k in range(4)]
    z = scores_of(sum_ref, edge_ref, row_ref, unit_ref, col_ref, held[0], held[1])
    row = node_row(z, held[0], held[1], held[2])
    total = kept_ref[...] + jnp.where(
        held[3] == 0, pltpu.roll(row, 32, 1), pltpu.roll(row, 40, 1)
    )
    out_ref[...] = jnp.broadcast_to(total[None], out_ref.shape)


def relax_kernel(place_ref, all_ref, scores_ref, positions_ref, hold_ref):
    sec, strip = place_ref[0], place_ref[1]
    strips = 4
    lane = lax.broadcasted_iota(jnp.int32, (8, LANES), 1)
    row = lax.broadcasted_iota(jnp.int32, (8, LANES), 0)
    seat = lane % 64
    slots = []
    for t in range(strips):
        block = all_ref[t * 64 : (t + 1) * 64, :]
        turned = jnp.concatenate([block, jnp.zeros((64, LANES), jnp.float32)], axis=0).T
        slots.append([turned[8 * n : 8 * n + 8] for n in range(6)])
    firsts, seconds = [], []
    for t in range(strips):
        for i in range(2):
            ahead = jnp.where(lane == 0, 0.0, pltpu.roll(slots[t][4 + i], 1, 1))
            firsts.append(slots[t][i] + ahead)
            seconds.append(slots[t][2 + i])

    def field(arrays, comp):
        return jnp.concatenate([a[comp : comp + 1] for a in arrays], axis=0)

    def both(low, high):
        return jnp.where(lane < 64, low, pltpu.roll(high, 64, 1))

    w_a = field(firsts, 0)
    w_a = jnp.where(lane == 0, 0.0, w_a)
    w_b = field(seconds, 0)
    w_a, w_b = both(w_a, w_a), both(w_b, w_b)
    o_a = both(field(firsts, 1), field(firsts, 2))
    o_b = both(field(seconds, 1), field(seconds, 2))
    drift_a = jnp.sum(w_a * o_a, axis=0, keepdims=True) / (
        jnp.sum(w_a, axis=0, keepdims=True) + 1.0
    )
    drift_b = jnp.sum(w_b * o_b, axis=0, keepdims=True) / (
        jnp.sum(w_b, axis=0, keepdims=True) + 1.0
    )
    drift_a = jnp.broadcast_to(drift_a, (8, LANES))
    drift_b = jnp.broadcast_to(drift_b, (8, LANES))
    run = drift_a + drift_b
    for shift in (1, 2, 4, 8, 16, 32):
        run = run + jnp.where(seat >= shift, pltpu.roll(run, shift, 1), 0.0)
    p_b = run
    p_a = run - drift_b

    def links(p):
        left = jnp.where(row > 0, pltpu.roll(p, 1, 0), p)
        right = jnp.where(row < 7, pltpu.roll(p, 7, 0), p)
        return (p - left) + (p - right)

    for _ in range(ITERS):
        e_a = w_a * (p_a - pltpu.roll(p_b, 1, 1) - o_a)
        e_b = w_b * (p_b - p_a - o_b)
        e_next = pltpu.roll(e_a, LANES - 1, 1)
        n_a = p_a - STEP_SIZE * (e_a - e_b + KAPPA * links(p_a))
        n_b = p_b - STEP_SIZE * (e_b - e_next + KAPPA * links(p_b))
        p_a, p_b = n_a, n_b
    for s, p in enumerate((p_a, p_b)):
        first = jnp.sum(jnp.where(lane == sec, p, 0.0), axis=1, keepdims=True)
        other = jnp.sum(jnp.where(lane == sec + 64, p, 0.0), axis=1, keepdims=True)
        hold_ref[s] = jnp.where(lane == 0, first, other)
        for i in range(2):
            positions_ref[s, i : i + 1, :] = hold_ref[s, pl.ds(2 * strip + i, 1), :][:, :2]
    own = all_ref[pl.ds(strip * 64 + sec, 1), :]
    earlier = all_ref[pl.ds(strip * 64 + jnp.maximum(sec - 1, 0), 1), :]
    earlier = jnp.where(sec > 0, earlier, 0.0)
    for i in range(2):
        value = pltpu.roll(own, LANES - (8 * i + 3), 1) + pltpu.roll(
            earlier, LANES - (32 + 8 * i + 3), 1
        )
        scores_ref[0, i : i + 1, :] = value[:, :5]
        scores_ref[1, i : i + 1, :] = pltpu.roll(own, LANES - (16 + 8 * i + 3), 1)[:, :5]


def body(features, intersection, peak_offsets, node_valid):
    secs, strips = lax.axis_size("sec"), lax.axis_size("strip")
    sec, strip = lax.axis_index("sec"), lax.axis_index("strip")
    columns, rows = (jnp.asarray(t) for t in tables())
    row_phase, unit_phase, col_phase = (jnp.asarray(t) for t in phase_tables())
    up = [(i, i + 1) for i in range(secs - 1)]
    down = [(i + 1, i) for i in range(secs - 1)]

    sent_down = noted_spectra(features, intersection, peak_offsets, node_valid, columns, rows)
    above = lax.ppermute(sent_down, "sec", down)
    sent_up = spectra(features, intersection, columns, rows, lambda n, meet: (1, 0, n), BATCHES)
    below = lax.ppermute(sent_up, "sec", up)

    def where(n, meet):
        late = n // BATCHES
        return late, jnp.where(late == 0, meet[0, 0, 0], 1), n % BATCHES

    rest = spectra(features, intersection, columns, rows, where, 2 * BATCHES)

    smem = pl.BlockSpec(memory_space=pltpu.SMEM)
    vmem = pl.BlockSpec(memory_space=pltpu.VMEM)
    row_shape = jax.ShapeDtypeStruct((1, LANES), jnp.float32)

    def call(kernel, in_specs, out_shape, pairs, *args):
        lead = (2,) if pairs == 2 else ()
        return pl.pallas_call(
            kernel,
            in_specs=in_specs,
            out_specs=vmem,
            out_shape=out_shape,
            scratch_shapes=[
                pltpu.VMEM(lead + (2, WIDTH, LANES), jnp.float32),
                pltpu.VMEM(lead + (2, 8, LANES), jnp.float32),
            ],
            compiler_params=pltpu.CompilerParams(vmem_limit_bytes=16 * 1024 * 1024),
            cost_estimate=pl.CostEstimate(
                flops=pairs * 32 * 25600 * 200, bytes_accessed=3400000 * pairs, transcendentals=0
            ),
        )(*args)

    local = call(
        local_kernel, [smem] * 3 + [vmem] * 6, row_shape, 2,
        intersection, peak_offsets, node_valid, sent_up, sent_down, rest,
        row_phase, unit_phase, col_phase,
    )
    kept = call(
        kept_kernel, [smem] * 3 + [vmem] * 6, row_shape, 1,
        intersection, peak_offsets, node_valid, rest, below, row_phase, unit_phase, col_phase, local,
    )
    total = secs * strips
    message = call(
        given_kernel, [vmem] * 6, jax.ShapeDtypeStruct((total, 1, LANES), jnp.float32), 1,
        rest, above, row_phase, unit_phase, col_phase, kept,
    )

    gathered = lax.all_to_all(message, ("strip", "sec"), 0, 0).reshape(strips, secs, LANES)
    if secs < 64:
        gathered = jnp.pad(gathered, ((0, 0), (0, 64 - secs), (0, 0)))
    gathered = gathered.reshape(strips * 64, LANES)
    scores, positions = pl.pallas_call(
        relax_kernel,
        in_specs=[smem, vmem],
        out_specs=[vmem, vmem],
        out_shape=[
            jax.ShapeDtypeStruct((2, 2, 5), jnp.float32),
            jax.ShapeDtypeStruct((2, 2, 2), jnp.float32),
        ],
        scratch_shapes=[pltpu.VMEM((2, 8, LANES), jnp.float32)],
        compiler_params=pltpu.CompilerParams(vmem_limit_bytes=4 * 1024 * 1024),
    )(jnp.stack([sec, strip]).astype(jnp.int32), gathered)
    return scores, positions


def solution(mesh):
    placed = (
        P("sec", "strip", None, None, None),
        P("sec", "strip", None),
        P("sec", "strip", None),
        P("sec", "strip"),
    )
    return jax.shard_map(
        body,
        mesh=mesh,
        in_specs=placed,
        out_specs=(P("sec", "strip", None), P("sec", "strip", None)),
        check_vma=False,
    )
```

```python
import functools
import math

import jax
import jax.numpy as jnp
import ml_dtypes
import numpy as np
from jax import lax
from jax.experimental import pallas as pl
from jax.experimental.pallas import tpu as pltpu
from jax.sharding import PartitionSpec as P

ITERS = 8
KAPPA = 1.0
STEP_SIZE = 0.2
UNIT_SCALE = 0.125

WIDTH = 160
HALF = 80
LANES = 128
BATCH = 8
GROUPS = 5
PACKED = GROUPS * LANES
CHANNELS = 32
BATCHES = CHANNELS // BATCH
REACH = 13
BLOCK = 2 * WIDTH
CROSS_UNROLL = 10
PER_STEP = 2
NOTE = 16

SHIFTS = [(HALF * i) % LANES for i in range(BATCH)]
PIECES = [
    [(80, 0), (128, 1)],
    [(32, 1), (112, 2), (128, 3)],
    [(64, 3), (128, 4)],
    [(16, 4), (96, 5), (128, 6)],
    [(48, 6), (128, 7)],
]
STARTS = [[0, 80], [32, 112], [64], [16, 96], [48]]
ROW_FREQ = np.concatenate([np.arange(HALF), [HALF], -np.arange(1, HALF)])


def angle(product):
    return 2.0 * math.pi / WIDTH * (product % WIDTH)


def tables():
    counter = np.arange(WIDTH)
    angles = angle(counter[:, None] * counter[None, :])
    cosine, sine = np.cos(angles), np.sin(angles)
    cos_part = cosine[:HALF]
    sin_part = np.concatenate([cosine[HALF : HALF + 1], sine[1:HALF]], axis=0)
    rows = np.concatenate([cos_part, sin_part], axis=0)
    columns = np.zeros((BATCH, WIDTH, 2 * LANES))
    for i, shift in enumerate(SHIFTS):
        lanes = (np.arange(HALF) + shift) % LANES
        columns[i][:, lanes] = cos_part.T
        columns[i][:, LANES + lanes] = sin_part.T
    return columns.astype(ml_dtypes.bfloat16), rows.astype(ml_dtypes.bfloat16)


def phase_tables():
    peaks = np.arange(-REACH, REACH + 1)
    rows = np.zeros((WIDTH, LANES))
    a = angle(ROW_FREQ[:, None] * peaks[None, :])
    rows[:, : len(peaks)] = np.cos(a)
    rows[:, 64 : 64 + len(peaks)] = np.sin(a)
    unit = np.zeros((2, WIDTH, LANES))
    unit[0] = np.cos(angle(ROW_FREQ))[:, None]
    unit[1] = np.sin(angle(ROW_FREQ))[:, None]
    columns = np.zeros((4, 32, LANES))
    low = np.arange(HALF)
    high = low.copy()
    high[0] = HALF
    for h, freq in enumerate((low, high)):
        b = angle(peaks[:, None] * freq[None, :])
        columns[2 * h, : len(peaks), :HALF] = np.cos(b)
        columns[2 * h + 1, : len(peaks), :HALF] = np.sin(b)
    return rows.astype(np.float32), unit.astype(np.float32), columns.astype(np.float32)


def transform(image, columns_ref, rows_ref, packed_ref, store):
    lane2 = lax.broadcasted_iota(jnp.int32, (1, 2 * LANES), 1) % LANES
    halves = {}

    def half(i):
        halves[i] = jnp.dot(image(i), columns_ref[i], preferred_element_type=jnp.float32)

    def pack(group):
        pieces = PIECES[group]
        value = halves[pieces[-1][1]]
        for end, i in pieces[-2::-1]:
            value = jnp.where(lane2 < end, halves[i], value)
        packed_ref[:, group * 2 * LANES : (group + 1) * 2 * LANES] = value.astype(jnp.bfloat16)

    lane = lax.broadcasted_iota(jnp.int32, (1, LANES), 1)
    edge = lax.broadcasted_iota(jnp.int32, (16, LANES), 0) == 0

    def finish(group):
        whole = jnp.dot(
            rows_ref[...],
            packed_ref[:, group * 2 * LANES : (group + 1) * 2 * LANES],
            preferred_element_type=jnp.float32,
        )
        first = lane == STARTS[group][0]
        for start in STARTS[group][1:]:
            first = first | (lane == start)
        cc, cs = whole[:HALF, :LANES], whole[:HALF, LANES:]
        sc, ss = whole[HALF:, :LANES], whole[HALF:, LANES:]
        ss0 = jnp.where(first, 0.0, ss)
        cs0 = jnp.where(first, 0.0, cs)
        values = [
            (0, 0, cc - ss0, cc),
            (0, 1, jnp.where(first, cs, cc + ss0), jnp.where(first, cs, sc)),
            (1, 0, -(cs0 + sc), jnp.where(first, -sc, -cs)),
            (1, 1, jnp.where(first, ss, sc - cs0), jnp.where(first, ss, -ss)),
        ]
        for c, h, value, fixed in values:
            top = jnp.where(edge, fixed[:16], value[:16]).astype(jnp.bfloat16)
            store(c, h * HALF, 16, group, top)
            store(c, h * HALF + 16, HALF - 16, group, value[16:].astype(jnp.bfloat16))

    half(0)
    half(1)
    pack(0)
    half(2)
    half(3)
    pack(1)
    finish(0)
    half(4)
    pack(2)
    finish(1)
    half(5)
    half(6)
    pack(3)
    finish(2)
    half(7)
    pack(4)
    finish(3)
    finish(4)


def spectra_kernel(*refs, where, count, noted, after):
    if noted:
        meet_ref, peak_ref, valid_ref, *refs = refs
    else:
        meet_ref, *refs = refs
    images_ref, columns_ref, rows_ref, *refs = refs
    out_ref, held_ref, packed_ref, sems = refs[1:] if after else refs

    def fetch(n):
        section, patch, batch = where(n, meet_ref)
        return pltpu.make_async_copy(
            images_ref.at[section, patch, pl.ds(batch * BATCH, BATCH)], held_ref.at[n], sems.at[n]
        )

    for n in range(count):
        fetch(n).start()

    def one(n, slot):
        fetch(n).wait()

        def store(c, row, size, group, value):
            at = pl.multiple_of(n * BLOCK + c * WIDTH + row, 16)
            out_ref[pl.ds(at, size), group * LANES : (group + 1) * LANES] = value

        transform(lambda i: held_ref[n, i], columns_ref, rows_ref, packed_ref.at[slot], store)

    def step(k, carry):
        for slot in range(PER_STEP):
            one(k * PER_STEP + slot, slot)
        return carry

    lax.fori_loop(0, count // PER_STEP, step, 0)

    if noted:
        give = 1 - meet_ref[0, 0, 0]
        lane = lax.broadcasted_iota(jnp.int32, (NOTE, PACKED), 1)
        note = jnp.zeros((NOTE, PACKED), jnp.float32)
        values = [peak_ref[0, give, 0], peak_ref[0, give, 1], valid_ref[0, give], give]
        for k, value in enumerate(values):
            note = jnp.where(lane == k, value.astype(jnp.float32), note)
        out_ref[count * BLOCK : count * BLOCK + NOTE, :] = note.astype(jnp.bfloat16)


def spectra(features, integers, columns, rows, where, count, noted, limit, after=()):
    smem = pl.BlockSpec(memory_space=pltpu.SMEM)
    vmem = pl.BlockSpec(memory_space=pltpu.VMEM)
    anywhere = pl.BlockSpec(memory_space=pl.ANY)
    return pl.pallas_call(
        functools.partial(
            spectra_kernel, where=where, count=count, noted=noted, after=bool(after)
        ),
        in_specs=[smem] * len(integers) + [anywhere, vmem, vmem] + [anywhere] * len(after),
        out_specs=vmem,
        out_shape=jax.ShapeDtypeStruct((count * BLOCK + noted, PACKED), jnp.bfloat16),
        scratch_shapes=[
            pltpu.VMEM((count, BATCH, WIDTH, WIDTH), jnp.bfloat16),
            pltpu.VMEM((PER_STEP, WIDTH, 2 * PACKED), jnp.bfloat16),
            pltpu.SemaphoreType.DMA((count,)),
        ],
        compiler_params=pltpu.CompilerParams(vmem_limit_bytes=limit * 1024 * 1024),
        cost_estimate=pl.CostEstimate(
            flops=count * BATCH * 2 * 2 * WIDTH * WIDTH,
            bytes_accessed=count * BATCH * 1400,
            transcendentals=0,
        ),
    )(*integers, features, columns, rows, *after)


def my_core():
    return lax.axis_index("sec") % 2


def gather_windows(g):
    lane = lax.broadcasted_iota(jnp.int32, (1, LANES), 1)
    low = lane < 80
    windows = [
        (80, jnp.where(low, g[1], g[0])),
        (32, g[1]),
        (112, jnp.where(lane < 112, g[2], g[1])),
        (64, jnp.where(lane < 64, g[3], g[2])),
        (16, g[3]),
        (96, jnp.where(lane < 96, g[4], g[3])),
        (48, g[4]),
    ]
    total = g[0]
    for shift, value in windows:
        total = total + pltpu.roll(value, LANES - shift, 1)
    return total


def cross_into(sum_ref, edge_ref, own, near, sign):
    def load(side, n, c, start, lanes):
        at = pl.multiple_of(side[1] + n * BLOCK + c * WIDTH + start, 16)
        return side[0][pl.ds(at, 16), lanes].astype(jnp.float32)

    def step(k, carry):
        start = pl.multiple_of(k * 16, 16)
        reals, imags = [], []
        for group in range(GROUPS):
            lanes = slice(group * LANES, (group + 1) * LANES)
            real = imag = None
            for n in range(BATCHES):
                own_re, own_im = (load(own, n, c, start, lanes) for c in range(2))
                near_re, near_im = (load(near, n, c, start, lanes) for c in range(2))
                re = own_re * near_re + own_im * near_im
                im = own_re * near_im - own_im * near_re
                real = re if real is None else real + re
                imag = im if imag is None else imag + im
            reals.append(real)
            imags.append(imag)
        sum_ref[0, pl.ds(start, 16), :] = gather_windows(reals)
        sum_ref[1, pl.ds(start, 16), :] = sign * gather_windows(imags)
        return carry

    lax.fori_loop(0, WIDTH // 16, step, 0, unroll=CROSS_UNROLL)
    for h in range(2):
        boths = []
        for group in range(GROUPS):
            lanes = slice(group * LANES, (group + 1) * LANES)
            both = None
            for n in range(BATCHES):
                ii = load(own, n, 1, h * HALF, lanes) * load(near, n, 1, h * HALF, lanes)
                both = ii if both is None else both + ii
            boths.append(both[:8])
        edge_ref[h] = gather_windows(boths)


def scores_of(sum_ref, edge_ref, row_ref, unit_ref, col_ref, peak_row, peak_col):
    lane = lax.broadcasted_iota(jnp.int32, (1, LANES), 1)
    damp = WIDTH * WIDTH * math.sqrt(CHANNELS)
    sums = {}
    moved = pltpu.roll(row_ref[...], (LANES - REACH) - peak_row, 1)
    for h in range(2):
        rows = slice(h * HALF, (h + 1) * HALF)
        real, imag = sum_ref[0, rows, :], sum_ref[1, rows, :]
        inverse = 1.0 / (jnp.sqrt(real * real + imag * imag) + damp)
        white_re, white_im = real * inverse, imag * inverse
        ii = edge_ref[h][0:1, :]
        rr = real[0:1, :] - ii
        z_rr = 0.5 * rr / (jnp.abs(rr) + damp)
        z_ii = 0.5 * ii / (jnp.abs(ii) + damp)
        stays, goes = (z_rr, z_ii) if h == 0 else (z_ii, z_rr)
        corner = (lax.broadcasted_iota(jnp.int32, (8, LANES), 0) == 0) & (
            lax.broadcasted_iota(jnp.int32, (8, LANES), 1) == 0
        )
        white_re = jnp.concatenate(
            [jnp.where(corner, jnp.broadcast_to(stays, (8, LANES)), white_re[:8]), white_re[8:]], 0
        )
        white_im = jnp.concatenate([jnp.where(corner, 0.0, white_im[:8]), white_im[8:]], 0)
        cos, sin = moved[rows, 0:1], moved[rows, 64:65]
        turned_re = white_re * cos - white_im * sin
        turned_im = white_re * sin + white_im * cos
        unit_cos, unit_sin = unit_ref[0, rows, :], unit_ref[1, rows, :]
        add = lambda x: jnp.sum(x, axis=0, keepdims=True)
        plain_re, plain_im = add(turned_re), add(turned_im)
        cos_re, cos_im = add(turned_re * unit_cos), add(turned_im * unit_cos)
        sin_re, sin_im = add(turned_re * unit_sin), add(turned_im * unit_sin)
        sums[h] = [
            (plain_re, plain_im),
            (cos_re + sin_im, cos_im - sin_re),
            (cos_re - sin_im, cos_im + sin_re),
        ]
        extra = jnp.where(lane == 0, goes, 0.0)
        for a in range(3):
            turn = moved[HALF : HALF + 1, 0:1] * (1.0 if a == 0 else -1.0) if h == 0 else 1.0
            sums[h][a] = (sums[h][a][0] + extra * turn, sums[h][a][1])
    out = []
    for a, b in ((0, 0), (1, 0), (2, 0), (0, -1), (0, 1)):
        total = None
        for h in range(2):
            cos = col_ref[2 * h, pl.ds(peak_col + (REACH + b), 1), :]
            sin = col_ref[2 * h + 1, pl.ds(peak_col + (REACH + b), 1), :]
            term = sums[h][a][0] * cos - sums[h][a][1] * sin
            total = term if total is None else total + term
        out.append(jnp.sum(total, axis=1, keepdims=True) * (4.0 / WIDTH))
    return out


def node_row(z, peak_row, peak_col, valid):
    lane = lax.broadcasted_iota(jnp.int32, (1, LANES), 1)
    wide = [jnp.broadcast_to(value, (1, LANES)) for value in z]
    spread_row = jnp.abs(wide[1]) + jnp.abs(wide[0]) + jnp.abs(wide[2]) + 1.0
    spread_col = jnp.abs(wide[3]) + jnp.abs(wide[0]) + jnp.abs(wide[4]) + 1.0
    off_row = UNIT_SCALE * (
        peak_row.astype(jnp.float32) + 0.5 * (wide[2] - wide[1]) / spread_row
    )
    off_col = UNIT_SCALE * (
        peak_col.astype(jnp.float32) + 0.5 * (wide[4] - wide[3]) / spread_col
    )
    weight = valid.astype(jnp.float32) * (1.0 + jnp.tanh(wide[0]))
    row = jnp.zeros((1, LANES), jnp.float32)
    for n, value in enumerate([weight, off_row, off_col] + wide):
        row = jnp.where(lane == n, value, row)
    return row


def local_kernel(
    meet_ref, peak_ref, valid_ref, far_ref, near_ref, rest_ref, row_ref, unit_ref, col_ref, out_ref,
    sum_ref, edge_ref,
):
    rest = BATCHES * BLOCK
    core = my_core()
    same = meet_ref[1, 0, 0] == 1 - meet_ref[0, 0, 0]

    @pl.when(same)
    def _():
        sign = jnp.where(core == 1, 1.0, -1.0)
        cross_into(sum_ref.at[0], edge_ref.at[0], (far_ref, 0), (near_ref, 0), sign)
        cross_into(sum_ref.at[1], edge_ref.at[1], (rest_ref, rest), (rest_ref, 0), 1.0)

    def apart(patch_ref, given_ref):
        cross_into(sum_ref.at[0], edge_ref.at[0], (patch_ref, 0), (rest_ref, 0), 1.0)
        cross_into(sum_ref.at[1], edge_ref.at[1], (rest_ref, rest), (given_ref, 0), 1.0)

    pl.when(jnp.logical_not(same) & (core == 1))(lambda: apart(far_ref, near_ref))
    pl.when(jnp.logical_not(same) & (core == 0))(lambda: apart(near_ref, far_ref))

    total = jnp.zeros((1, LANES), jnp.float32)
    for n in range(2):
        peak = peak_ref[1, n, 0], peak_ref[1, n, 1]
        z = scores_of(sum_ref.at[n], edge_ref.at[n], row_ref, unit_ref, col_ref, *peak)
        total = total + pltpu.roll(node_row(z, *peak, valid_ref[1, n]), 16 + 8 * n, 1)
    out_ref[...] = total


def met_kernel(
    meet_ref, peak_ref, valid_ref, rest_ref, got_ref, row_ref, unit_ref, col_ref, before_ref,
    out_ref, sum_ref, edge_ref, *, far,
):
    after = my_core() == (1 if far else 0)
    keep = meet_ref[0, 0, 0]
    note = got_ref[BATCHES * BLOCK : BATCHES * BLOCK + NOTE, :LANES].astype(jnp.float32)[0:1, :]
    lane = lax.broadcasted_iota(jnp.int32, (1, LANES), 1)
    held = [jnp.sum(jnp.where(lane == k, note, 0.0)).astype(jnp.int32) for k in range(4)]
    peak_row = jnp.where(after, held[0], peak_ref[0, keep, 0])
    peak_col = jnp.where(after, held[1], peak_ref[0, keep, 1])
    valid = jnp.where(after, held[2], valid_ref[0, keep])
    place = jnp.where(after, 32 + 8 * held[3], 8 * keep)
    start = jnp.where(after, BATCHES * BLOCK, 0)
    sign = jnp.where(after, -1.0, 1.0)
    cross_into(sum_ref, edge_ref, (rest_ref, start), (got_ref, 0), sign)
    z = scores_of(sum_ref, edge_ref, row_ref, unit_ref, col_ref, peak_row, peak_col)
    row = node_row(z, peak_row, peak_col, valid)
    total = before_ref[...] + pltpu.roll(row, place, 1)
    out_ref[...] = jnp.broadcast_to(total, (1, LANES)) if not far else jnp.broadcast_to(
        total[None], out_ref.shape
    )


def relax_kernel(all_ref, scores_ref, positions_ref, hold_ref):
    sec, strip = lax.axis_index("sec"), lax.axis_index("strip")
    strips = 4
    lane = lax.broadcasted_iota(jnp.int32, (8, LANES), 1)
    row = lax.broadcasted_iota(jnp.int32, (8, LANES), 0)
    seat = lane % 64
    slots = []
    for t in range(strips):
        block = all_ref[t * 64 : (t + 1) * 64, :]
        turned = jnp.concatenate([block, jnp.zeros((64, LANES), jnp.float32)], axis=0).T
        slots.append([turned[8 * n : 8 * n + 8] for n in range(6)])
    firsts, seconds = [], []
    for t in range(strips):
        for i in range(2):
            ahead = jnp.where(lane == 0, 0.0, pltpu.roll(slots[t][4 + i], 1, 1))
            firsts.append(slots[t][i] + ahead)
            seconds.append(slots[t][2 + i])

    def field(arrays, comp):
        return jnp.concatenate([a[comp : comp + 1] for a in arrays], axis=0)

    def both(low, high):
        return jnp.where(lane < 64, low, pltpu.roll(high, 64, 1))

    w_a = field(firsts, 0)
    w_a = jnp.where(lane == 0, 0.0, w_a)
    w_b = field(seconds, 0)
    w_a, w_b = both(w_a, w_a), both(w_b, w_b)
    o_a = both(field(firsts, 1), field(firsts, 2))
    o_b = both(field(seconds, 1), field(seconds, 2))
    drift_a = jnp.sum(w_a * o_a, axis=0, keepdims=True) / (
        jnp.sum(w_a, axis=0, keepdims=True) + 1.0
    )
    drift_b = jnp.sum(w_b * o_b, axis=0, keepdims=True) / (
        jnp.sum(w_b, axis=0, keepdims=True) + 1.0
    )
    drift_a = jnp.broadcast_to(drift_a, (8, LANES))
    drift_b = jnp.broadcast_to(drift_b, (8, LANES))
    run = drift_a + drift_b
    for shift in (1, 2, 4, 8, 16, 32):
        run = run + jnp.where(seat >= shift, pltpu.roll(run, shift, 1), 0.0)
    p_b = run
    p_a = run - drift_b

    def links(p):
        left = jnp.where(row > 0, pltpu.roll(p, 1, 0), p)
        right = jnp.where(row < 7, pltpu.roll(p, 7, 0), p)
        return (p - left) + (p - right)

    for _ in range(ITERS):
        e_a = w_a * (p_a - pltpu.roll(p_b, 1, 1) - o_a)
        e_b = w_b * (p_b - p_a - o_b)
        e_next = pltpu.roll(e_a, LANES - 1, 1)
        n_a = p_a - STEP_SIZE * (e_a - e_b + KAPPA * links(p_a))
        n_b = p_b - STEP_SIZE * (e_b - e_next + KAPPA * links(p_b))
        p_a, p_b = n_a, n_b
    for s, p in enumerate((p_a, p_b)):
        first = jnp.sum(jnp.where(lane == sec, p, 0.0), axis=1, keepdims=True)
        other = jnp.sum(jnp.where(lane == sec + 64, p, 0.0), axis=1, keepdims=True)
        hold_ref[s] = jnp.where(lane == 0, first, other)
        for i in range(2):
            positions_ref[s, i : i + 1, :] = hold_ref[s, pl.ds(2 * strip + i, 1), :][:, :2]
    own = all_ref[pl.ds(strip * 64 + sec, 1), :]
    earlier = all_ref[pl.ds(strip * 64 + jnp.maximum(sec - 1, 0), 1), :]
    earlier = jnp.where(sec > 0, earlier, 0.0)
    for i in range(2):
        value = pltpu.roll(own, LANES - (8 * i + 3), 1) + pltpu.roll(
            earlier, LANES - (32 + 8 * i + 3), 1
        )
        scores_ref[0, i : i + 1, :] = value[:, :5]
        scores_ref[1, i : i + 1, :] = pltpu.roll(own, LANES - (16 + 8 * i + 3), 1)[:, :5]


def sent_place(n, meet_ref, far):
    up = (my_core() == 1) == far
    return jnp.where(up, 1, 0), jnp.where(up, 0, 1 - meet_ref[0, 0, 0]), n


def rest_place(n, meet_ref):
    late = n // BATCHES
    return late, jnp.where(late == 0, meet_ref[0, 0, 0], 1), n % BATCHES


def body(features, intersection, peak_offsets, node_valid):
    secs, strips = lax.axis_size("sec"), lax.axis_size("strip")
    columns, rows = (jnp.asarray(t) for t in tables())
    row_phase, unit_phase, col_phase = (jnp.asarray(t) for t in phase_tables())
    integers = (intersection, peak_offsets, node_valid)

    def swap(first):
        pairs = [(i, i + 1) for i in range(first, secs - 1, 2)]
        return pairs + [(b, a) for a, b in pairs]

    sent_far = spectra(
        features, integers, columns, rows, functools.partial(sent_place, far=True), BATCHES, 2 * NOTE, 50
    )
    got_far = lax.ppermute(sent_far, "sec", swap(1))
    sent_near = spectra(
        features, integers, columns, rows, functools.partial(sent_place, far=False), BATCHES, NOTE, 50,
        (sent_far,),
    )
    got_near = lax.ppermute(sent_near, "sec", swap(0))
    rest = spectra(
        features, (intersection,), columns, rows, rest_place, 2 * BATCHES, 0, 44, (sent_near,)
    )

    smem = pl.BlockSpec(memory_space=pltpu.SMEM)
    vmem = pl.BlockSpec(memory_space=pltpu.VMEM)
    row_shape = jax.ShapeDtypeStruct((1, LANES), jnp.float32)

    def call(kernel, in_specs, out_shape, pairs, *args):
        lead = (2,) if pairs == 2 else ()
        return pl.pallas_call(
            kernel,
            in_specs=in_specs,
            out_specs=vmem,
            out_shape=out_shape,
            scratch_shapes=[
                pltpu.VMEM(lead + (2, WIDTH, LANES), jnp.float32),
                pltpu.VMEM(lead + (2, 8, LANES), jnp.float32),
            ],
            compiler_params=pltpu.CompilerParams(vmem_limit_bytes=16 * 1024 * 1024),
            cost_estimate=pl.CostEstimate(
                flops=1, bytes_accessed=1, transcendentals=0
            ),
        )(*args)

    phases = (row_phase, unit_phase, col_phase)
    local = call(
        local_kernel, [smem] * 3 + [vmem] * 6, row_shape, 2, *integers, sent_far, sent_near, rest, *phases
    )
    near = call(
        functools.partial(met_kernel, far=False), [smem] * 3 + [vmem] * 6, row_shape, 1,
        *integers, rest, got_near, *phases, local,
    )
    message = call(
        functools.partial(met_kernel, far=True), [smem] * 3 + [vmem] * 6,
        jax.ShapeDtypeStruct((secs * strips, 1, LANES), jnp.float32), 1,
        *integers, rest, got_far, *phases, near,
    )

    gathered = lax.all_to_all(message, ("strip", "sec"), 0, 0).reshape(strips, secs, LANES)
    if secs < 64:
        gathered = jnp.pad(gathered, ((0, 0), (0, 64 - secs), (0, 0)))
    gathered = gathered.reshape(strips * 64, LANES)
    scores, positions = pl.pallas_call(
        relax_kernel,
        in_specs=[vmem],
        out_specs=[vmem, vmem],
        out_shape=[
            jax.ShapeDtypeStruct((2, 2, 5), jnp.float32),
            jax.ShapeDtypeStruct((2, 2, 2), jnp.float32),
        ],
        scratch_shapes=[pltpu.VMEM((2, 8, LANES), jnp.float32)],
        compiler_params=pltpu.CompilerParams(vmem_limit_bytes=4 * 1024 * 1024),
    )(gathered)
    return scores, positions


def solution(mesh):
    placed = (
        P("sec", "strip", None, None, None),
        P("sec", "strip", None),
        P("sec", "strip", None),
        P("sec", "strip"),
    )
    return jax.shard_map(
        body,
        mesh=mesh,
        in_specs=placed,
        out_specs=(P("sec", "strip", None), P("sec", "strip", None)),
        check_vma=False,
    )
```

```python
import functools
import math

import jax
import jax.numpy as jnp
import ml_dtypes
import numpy as np
from jax import lax
from jax.experimental import pallas as pl
from jax.experimental.pallas import tpu as pltpu
from jax.sharding import PartitionSpec as P

ITERS = 8
KAPPA = 1.0
STEP_SIZE = 0.2
UNIT_SCALE = 0.125

WIDTH = 160
HALF = 80
LANES = 128
BATCH = 8
GROUPS = 5
PACKED = GROUPS * LANES
CHANNELS = 32
BATCHES = CHANNELS // BATCH
REACH = 13
BLOCK = 2 * WIDTH
CROSS_UNROLL = 10
SCORES = 72
PER_STEP = 2
NOTE = 16

SHIFTS = [(HALF * i) % LANES for i in range(BATCH)]
PIECES = [
    [(80, 0), (128, 1)],
    [(32, 1), (112, 2), (128, 3)],
    [(64, 3), (128, 4)],
    [(16, 4), (96, 5), (128, 6)],
    [(48, 6), (128, 7)],
]
STARTS = [[0, 80], [32, 112], [64], [16, 96], [48]]
ROW_FREQ = np.concatenate([np.arange(HALF), [HALF], -np.arange(1, HALF)])


def angle(product):
    return 2.0 * math.pi / WIDTH * (product % WIDTH)


def tables():
    counter = np.arange(WIDTH)
    angles = angle(counter[:, None] * counter[None, :])
    cosine, sine = np.cos(angles), np.sin(angles)
    cos_part = cosine[:HALF]
    sin_part = np.concatenate([cosine[HALF : HALF + 1], sine[1:HALF]], axis=0)
    rows = np.concatenate([cos_part, sin_part], axis=0)
    columns = np.zeros((BATCH, WIDTH, 2 * LANES))
    for i, shift in enumerate(SHIFTS):
        lanes = (np.arange(HALF) + shift) % LANES
        columns[i][:, lanes] = cos_part.T
        columns[i][:, LANES + lanes] = sin_part.T
    return columns.astype(ml_dtypes.bfloat16), rows.astype(ml_dtypes.bfloat16)


def phase_tables():
    peaks = np.arange(-REACH, REACH + 1)
    rows = np.zeros((WIDTH, LANES))
    a = angle(ROW_FREQ[:, None] * peaks[None, :])
    rows[:, : len(peaks)] = np.cos(a)
    rows[:, 64 : 64 + len(peaks)] = np.sin(a)
    unit = np.zeros((2, WIDTH, LANES))
    unit[0] = np.cos(angle(ROW_FREQ))[:, None]
    unit[1] = np.sin(angle(ROW_FREQ))[:, None]
    columns = np.zeros((4, 32, LANES))
    low = np.arange(HALF)
    high = low.copy()
    high[0] = HALF
    for h, freq in enumerate((low, high)):
        b = angle(peaks[:, None] * freq[None, :])
        columns[2 * h, : len(peaks), :HALF] = np.cos(b)
        columns[2 * h + 1, : len(peaks), :HALF] = np.sin(b)
    return rows.astype(np.float32), unit.astype(np.float32), columns.astype(np.float32)


def transform(image, columns_ref, rows_ref, packed_ref, store):
    lane2 = lax.broadcasted_iota(jnp.int32, (1, 2 * LANES), 1) % LANES
    halves = {}

    def half(i):
        halves[i] = jnp.dot(image(i), columns_ref[i], preferred_element_type=jnp.float32)

    def pack(group):
        pieces = PIECES[group]
        value = halves[pieces[-1][1]]
        for end, i in pieces[-2::-1]:
            value = jnp.where(lane2 < end, halves[i], value)
        packed_ref[:, group * 2 * LANES : (group + 1) * 2 * LANES] = value.astype(jnp.bfloat16)

    lane = lax.broadcasted_iota(jnp.int32, (1, LANES), 1)
    edge = lax.broadcasted_iota(jnp.int32, (16, LANES), 0) == 0

    def finish(group):
        whole = jnp.dot(
            rows_ref[...],
            packed_ref[:, group * 2 * LANES : (group + 1) * 2 * LANES],
            preferred_element_type=jnp.float32,
        )
        first = lane == STARTS[group][0]
        for start in STARTS[group][1:]:
            first = first | (lane == start)
        cc, cs = whole[:HALF, :LANES], whole[:HALF, LANES:]
        sc, ss = whole[HALF:, :LANES], whole[HALF:, LANES:]
        ss0 = jnp.where(first, 0.0, ss)
        cs0 = jnp.where(first, 0.0, cs)
        values = [
            (0, 0, cc - ss0, cc),
            (0, 1, jnp.where(first, cs, cc + ss0), jnp.where(first, cs, sc)),
            (1, 0, -(cs0 + sc), jnp.where(first, -sc, -cs)),
            (1, 1, jnp.where(first, ss, sc - cs0), jnp.where(first, ss, -ss)),
        ]
        for c, h, value, fixed in values:
            top = jnp.where(edge, fixed[:16], value[:16]).astype(jnp.bfloat16)
            store(c, h * HALF, 16, group, top)
            store(c, h * HALF + 16, HALF - 16, group, value[16:].astype(jnp.bfloat16))

    half(0)
    half(1)
    pack(0)
    half(2)
    half(3)
    pack(1)
    finish(0)
    half(4)
    pack(2)
    finish(1)
    half(5)
    half(6)
    pack(3)
    finish(2)
    half(7)
    pack(4)
    finish(3)
    finish(4)


def spectra_kernel(*refs, where, count, noted, after):
    meet_in, peaks_in, valids_in, images_ref, columns_in, rows_in, *refs = refs
    refs = refs[1:] if after else refs
    out_ref, held_ref, packed_ref, columns_ref, rows_ref, *refs = refs
    meet_ref, peaks_ref, valids_ref, sems, other_sems = refs

    def fetch(n):
        section, patch, batch = where(n, meet_ref)
        return pltpu.make_async_copy(
            images_ref.at[section, patch, pl.ds(batch * BATCH, BATCH)], held_ref.at[n], sems.at[n]
        )

    meet = pltpu.make_async_copy(meet_in, meet_ref, other_sems.at[0])
    meet.start()
    others = [
        pltpu.make_async_copy(columns_in, columns_ref, other_sems.at[1]),
        pltpu.make_async_copy(rows_in, rows_ref, other_sems.at[2]),
    ]
    if noted:
        others.append(pltpu.make_async_copy(peaks_in, peaks_ref, other_sems.at[3]))
        others.append(pltpu.make_async_copy(valids_in, valids_ref, other_sems.at[4]))
    for other in others:
        other.start()
    meet.wait()
    for n in range(count):
        fetch(n).start()
    for other in others:
        other.wait()

    def one(n, slot):
        fetch(n).wait()

        def store(c, row, size, group, value):
            at = pl.multiple_of(n * BLOCK + c * WIDTH + row, 16)
            out_ref[pl.ds(at, size), group * LANES : (group + 1) * LANES] = value

        transform(lambda i: held_ref[n, i], columns_ref, rows_ref, packed_ref.at[slot], store)

    def step(k, carry):
        for slot in range(PER_STEP):
            one(k * PER_STEP + slot, slot)
        return carry

    lax.fori_loop(0, count // PER_STEP, step, 0)

    if noted:
        give = 1 - meet_ref[0, 0, 0]
        lane = lax.broadcasted_iota(jnp.int32, (NOTE, PACKED), 1)
        note = jnp.zeros((NOTE, PACKED), jnp.float32)
        values = [peaks_ref[0, give, 0], peaks_ref[0, give, 1], valids_ref[0, give], give]
        for k, value in enumerate(values):
            note = jnp.where(lane == k, value.astype(jnp.float32), note)
        out_ref[count * BLOCK : count * BLOCK + NOTE, :] = note.astype(jnp.bfloat16)


def spectra(features, integers, columns, rows, where, count, noted, limit, after=()):
    vmem = pl.BlockSpec(memory_space=pltpu.VMEM)
    anywhere = pl.BlockSpec(memory_space=pl.ANY)
    hbm = pl.BlockSpec(memory_space=pltpu.HBM)
    return pl.pallas_call(
        functools.partial(
            spectra_kernel, where=where, count=count, noted=noted, after=bool(after)
        ),
        in_specs=[hbm] * 6 + [anywhere] * len(after),
        out_specs=vmem,
        out_shape=jax.ShapeDtypeStruct((count * BLOCK + noted, PACKED), jnp.bfloat16),
        scratch_shapes=[
            pltpu.VMEM((count, BATCH, WIDTH, WIDTH), jnp.bfloat16),
            pltpu.VMEM((PER_STEP, WIDTH, 2 * PACKED), jnp.bfloat16),
            pltpu.VMEM(columns.shape, jnp.bfloat16),
            pltpu.VMEM(rows.shape, jnp.bfloat16),
            pltpu.SMEM(integers[0].shape, jnp.int32),
            pltpu.SMEM(integers[1].shape, jnp.int32),
            pltpu.SMEM(integers[2].shape, jnp.int32),
            pltpu.SemaphoreType.DMA((count,)),
            pltpu.SemaphoreType.DMA((5,)),
        ],
        compiler_params=pltpu.CompilerParams(vmem_limit_bytes=limit * 1024 * 1024),
        cost_estimate=pl.CostEstimate(
            flops=count * BATCH * 2 * 2 * WIDTH * WIDTH,
            bytes_accessed=count * BATCH * 1400,
            transcendentals=0,
        ),
    )(*(pltpu.with_memory_space_constraint(a, pltpu.HBM) for a in (*integers, features, columns, rows)), *after)


def my_core():
    return lax.axis_index("sec") % 2


def gather_windows(g):
    lane = lax.broadcasted_iota(jnp.int32, (1, LANES), 1)
    low = lane < 80
    windows = [
        (80, jnp.where(low, g[1], g[0])),
        (32, g[1]),
        (112, jnp.where(lane < 112, g[2], g[1])),
        (64, jnp.where(lane < 64, g[3], g[2])),
        (16, g[3]),
        (96, jnp.where(lane < 96, g[4], g[3])),
        (48, g[4]),
    ]
    total = g[0]
    for shift, value in windows:
        total = total + pltpu.roll(value, LANES - shift, 1)
    return total


def cross_into(sum_ref, edge_ref, own, near, sign):
    def load(side, n, c, start, lanes):
        at = pl.multiple_of(side[1] + n * BLOCK + c * WIDTH + start, 16)
        return side[0][pl.ds(at, 16), lanes].astype(jnp.float32)

    def step(k, carry):
        start = pl.multiple_of(k * 16, 16)
        reals, imags = [], []
        for group in range(GROUPS):
            lanes = slice(group * LANES, (group + 1) * LANES)
            real = imag = None
            for n in range(BATCHES):
                own_re, own_im = (load(own, n, c, start, lanes) for c in range(2))
                near_re, near_im = (load(near, n, c, start, lanes) for c in range(2))
                re = own_re * near_re + own_im * near_im
                im = own_re * near_im - own_im * near_re
                real = re if real is None else real + re
                imag = im if imag is None else imag + im
            reals.append(real)
            imags.append(imag)
        sum_ref[0, pl.ds(start, 16), :] = gather_windows(reals)
        sum_ref[1, pl.ds(start, 16), :] = sign * gather_windows(imags)
        return carry

    lax.fori_loop(0, WIDTH // 16, step, 0, unroll=CROSS_UNROLL)
    for h in range(2):
        boths = []
        for group in range(GROUPS):
            lanes = slice(group * LANES, (group + 1) * LANES)
            both = None
            for n in range(BATCHES):
                ii = load(own, n, 1, h * HALF, lanes) * load(near, n, 1, h * HALF, lanes)
                both = ii if both is None else both + ii
            boths.append(both[:8])
        edge_ref[h] = gather_windows(boths)


def scores_of(sum_ref, edge_ref, row_ref, unit_ref, col_ref, peak_row, peak_col):
    lane = lax.broadcasted_iota(jnp.int32, (1, LANES), 1)
    damp = WIDTH * WIDTH * math.sqrt(CHANNELS)
    sums = {}
    moved = pltpu.roll(row_ref[...], (LANES - REACH) - peak_row, 1)
    for h in range(2):
        rows = slice(h * HALF, (h + 1) * HALF)
        real, imag = sum_ref[0, rows, :], sum_ref[1, rows, :]
        inverse = 1.0 / (jnp.sqrt(real * real + imag * imag) + damp)
        white_re, white_im = real * inverse, imag * inverse
        ii = edge_ref[h][0:1, :]
        rr = real[0:1, :] - ii
        z_rr = 0.5 * rr / (jnp.abs(rr) + damp)
        z_ii = 0.5 * ii / (jnp.abs(ii) + damp)
        stays, goes = (z_rr, z_ii) if h == 0 else (z_ii, z_rr)
        corner = (lax.broadcasted_iota(jnp.int32, (8, LANES), 0) == 0) & (
            lax.broadcasted_iota(jnp.int32, (8, LANES), 1) == 0
        )
        white_re = jnp.concatenate(
            [jnp.where(corner, jnp.broadcast_to(stays, (8, LANES)), white_re[:8]), white_re[8:]], 0
        )
        white_im = jnp.concatenate([jnp.where(corner, 0.0, white_im[:8]), white_im[8:]], 0)
        cos, sin = moved[rows, 0:1], moved[rows, 64:65]
        turned_re = white_re * cos - white_im * sin
        turned_im = white_re * sin + white_im * cos
        unit_cos, unit_sin = unit_ref[0, rows, :], unit_ref[1, rows, :]
        add = lambda x: jnp.sum(x, axis=0, keepdims=True)
        plain_re, plain_im = add(turned_re), add(turned_im)
        cos_re, cos_im = add(turned_re * unit_cos), add(turned_im * unit_cos)
        sin_re, sin_im = add(turned_re * unit_sin), add(turned_im * unit_sin)
        sums[h] = [
            (plain_re, plain_im),
            (cos_re + sin_im, cos_im - sin_re),
            (cos_re - sin_im, cos_im + sin_re),
        ]
        extra = jnp.where(lane == 0, goes, 0.0)
        for a in range(3):
            turn = moved[HALF : HALF + 1, 0:1] * (1.0 if a == 0 else -1.0) if h == 0 else 1.0
            sums[h][a] = (sums[h][a][0] + extra * turn, sums[h][a][1])
    out = []
    for a, b in ((0, 0), (1, 0), (2, 0), (0, -1), (0, 1)):
        total = None
        for h in range(2):
            cos = col_ref[2 * h, pl.ds(peak_col + (REACH + b), 1), :]
            sin = col_ref[2 * h + 1, pl.ds(peak_col + (REACH + b), 1), :]
            term = sums[h][a][0] * cos - sums[h][a][1] * sin
            total = term if total is None else total + term
        out.append(jnp.sum(total, axis=1, keepdims=True) * (4.0 / WIDTH))
    return out


def node_row(z, peak_row, peak_col, valid, kind, side):
    lane = lax.broadcasted_iota(jnp.int32, (1, LANES), 1)
    wide = [jnp.broadcast_to(value, (1, LANES)) for value in z]
    spread_row = jnp.abs(wide[1]) + jnp.abs(wide[0]) + jnp.abs(wide[2]) + 1.0
    spread_col = jnp.abs(wide[3]) + jnp.abs(wide[0]) + jnp.abs(wide[4]) + 1.0
    off_row = UNIT_SCALE * (
        peak_row.astype(jnp.float32) + 0.5 * (wide[2] - wide[1]) / spread_row
    )
    off_col = UNIT_SCALE * (
        peak_col.astype(jnp.float32) + 0.5 * (wide[4] - wide[3]) / spread_col
    )
    weight = valid.astype(jnp.float32) * (1.0 + jnp.tanh(wide[0]))
    first = 24 * kind + 2 * lax.axis_index("strip") + side
    row = jnp.zeros((1, LANES), jnp.float32)
    for n, value in enumerate([weight, off_row, off_col]):
        row = jnp.where(lane == first + 8 * n, value, row)
    for n, value in enumerate(wide):
        row = jnp.where(lane == SCORES + 10 * kind + 5 * side + n, value, row)
    return row


def local_kernel(
    meet_ref, peak_ref, valid_ref, far_ref, near_ref, rest_ref, row_ref, unit_ref, col_ref, out_ref,
    sum_ref, edge_ref,
):
    rest = BATCHES * BLOCK
    core = my_core()
    same = meet_ref[1, 0, 0] == 1 - meet_ref[0, 0, 0]

    @pl.when(same)
    def _():
        sign = jnp.where(core == 1, 1.0, -1.0)
        cross_into(sum_ref.at[0], edge_ref.at[0], (far_ref, 0), (near_ref, 0), sign)
        cross_into(sum_ref.at[1], edge_ref.at[1], (rest_ref, rest), (rest_ref, 0), 1.0)

    def apart(patch_ref, given_ref):
        cross_into(sum_ref.at[0], edge_ref.at[0], (patch_ref, 0), (rest_ref, 0), 1.0)
        cross_into(sum_ref.at[1], edge_ref.at[1], (rest_ref, rest), (given_ref, 0), 1.0)

    pl.when(jnp.logical_not(same) & (core == 1))(lambda: apart(far_ref, near_ref))
    pl.when(jnp.logical_not(same) & (core == 0))(lambda: apart(near_ref, far_ref))

    total = jnp.zeros((1, LANES), jnp.float32)
    for n in range(2):
        peak = peak_ref[1, n, 0], peak_ref[1, n, 1]
        z = scores_of(sum_ref.at[n], edge_ref.at[n], row_ref, unit_ref, col_ref, *peak)
        total = total + node_row(z, *peak, valid_ref[1, n], 1, n)
    out_ref[...] = total


def met_kernel(
    meet_ref, peak_ref, valid_ref, rest_ref, got_ref, row_ref, unit_ref, col_ref, before_ref,
    out_ref, sum_ref, edge_ref, *, far,
):
    after = my_core() == (1 if far else 0)
    keep = meet_ref[0, 0, 0]
    note = got_ref[BATCHES * BLOCK : BATCHES * BLOCK + NOTE, :LANES].astype(jnp.float32)[0:1, :]
    lane = lax.broadcasted_iota(jnp.int32, (1, LANES), 1)
    held = [jnp.sum(jnp.where(lane == k, note, 0.0)).astype(jnp.int32) for k in range(4)]
    peak_row = jnp.where(after, held[0], peak_ref[0, keep, 0])
    peak_col = jnp.where(after, held[1], peak_ref[0, keep, 1])
    valid = jnp.where(after, held[2], valid_ref[0, keep])
    kind = jnp.where(after, 2, 0)
    side = jnp.where(after, held[3], keep)
    start = jnp.where(after, BATCHES * BLOCK, 0)
    sign = jnp.where(after, -1.0, 1.0)
    cross_into(sum_ref, edge_ref, (rest_ref, start), (got_ref, 0), sign)
    z = scores_of(sum_ref, edge_ref, row_ref, unit_ref, col_ref, peak_row, peak_col)
    total = before_ref[...] + node_row(z, peak_row, peak_col, valid, kind, side)
    out_ref[...] = jnp.broadcast_to(total, (1, LANES)) if not far else jnp.broadcast_to(
        total[None], out_ref.shape
    )


def relax_kernel(all_ref, scores_ref, positions_ref, hold_ref):
    sec, strip = lax.axis_index("sec"), lax.axis_index("strip")
    strips = 4
    lane = lax.broadcasted_iota(jnp.int32, (8, LANES), 1)
    row = lax.broadcasted_iota(jnp.int32, (8, LANES), 0)
    seat = lane % 64
    blocks = [all_ref[t * 64 : (t + 1) * 64, :] for t in range(strips)]
    joined = (blocks[0] + blocks[1]) + (blocks[2] + blocks[3])
    turned = jnp.concatenate([joined, jnp.zeros((64, LANES), jnp.float32)], axis=0).T

    def field(n):
        return turned[8 * n : 8 * n + 8]

    def both(low, high):
        return jnp.where(lane < 64, low, pltpu.roll(high, 64, 1))

    def first(n):
        return field(n) + jnp.where(lane == 0, 0.0, pltpu.roll(field(6 + n), 1, 1))

    w_a = jnp.where(lane == 0, 0.0, first(0))
    w_a, w_b = both(w_a, w_a), both(field(3), field(3))
    o_a = both(first(1), first(2))
    o_b = both(field(4), field(5))
    drift_a = jnp.sum(w_a * o_a, axis=0, keepdims=True) / (
        jnp.sum(w_a, axis=0, keepdims=True) + 1.0
    )
    drift_b = jnp.sum(w_b * o_b, axis=0, keepdims=True) / (
        jnp.sum(w_b, axis=0, keepdims=True) + 1.0
    )
    drift_a = jnp.broadcast_to(drift_a, (8, LANES))
    drift_b = jnp.broadcast_to(drift_b, (8, LANES))
    run = drift_a + drift_b
    for shift in (1, 2, 4, 8, 16, 32):
        run = run + jnp.where(seat >= shift, pltpu.roll(run, shift, 1), 0.0)
    p_b = run
    p_a = run - drift_b

    def links(p):
        left = jnp.where(row > 0, pltpu.roll(p, 1, 0), p)
        right = jnp.where(row < 7, pltpu.roll(p, 7, 0), p)
        return (p - left) + (p - right)

    w_next = pltpu.roll(w_a, LANES - 1, 1)
    o_next = pltpu.roll(o_a, LANES - 1, 1)
    for _ in range(ITERS):
        before = pltpu.roll(p_b, 1, 1)
        after = pltpu.roll(p_a, LANES - 1, 1)
        e_a = w_a * (p_a - before - o_a)
        e_b = w_b * (p_b - p_a - o_b)
        e_next = w_next * (after - p_b - o_next)
        n_a = p_a - STEP_SIZE * (e_a - e_b + KAPPA * links(p_a))
        n_b = p_b - STEP_SIZE * (e_b - e_next + KAPPA * links(p_b))
        p_a, p_b = n_a, n_b
    for s, p in enumerate((p_a, p_b)):
        first = jnp.sum(jnp.where(lane == sec, p, 0.0), axis=1, keepdims=True)
        other = jnp.sum(jnp.where(lane == sec + 64, p, 0.0), axis=1, keepdims=True)
        hold_ref[s] = jnp.where(lane == 0, first, other)
        for i in range(2):
            positions_ref[s, i : i + 1, :] = hold_ref[s, pl.ds(2 * strip + i, 1), :][:, :2]
    own = all_ref[pl.ds(strip * 64 + sec, 1), :]
    earlier = all_ref[pl.ds(strip * 64 + jnp.maximum(sec - 1, 0), 1), :]
    earlier = jnp.where(sec > 0, earlier, 0.0)
    for i in range(2):
        shift = LANES - SCORES - 5 * i
        value = pltpu.roll(own, shift, 1) + pltpu.roll(earlier, shift - 20, 1)
        scores_ref[0, i : i + 1, :] = value[:, :5]
        scores_ref[1, i : i + 1, :] = pltpu.roll(own, shift - 10, 1)[:, :5]


def sent_place(n, meet_ref, far):
    up = (my_core() == 1) == far
    return jnp.where(up, 1, 0), jnp.where(up, 0, 1 - meet_ref[0, 0, 0]), n


def rest_place(n, meet_ref):
    late = n // BATCHES
    return late, jnp.where(late == 0, meet_ref[0, 0, 0], 1), n % BATCHES


def body(features, intersection, peak_offsets, node_valid):
    secs, strips = lax.axis_size("sec"), lax.axis_size("strip")
    columns, rows = (jnp.asarray(t) for t in tables())
    row_phase, unit_phase, col_phase = (jnp.asarray(t) for t in phase_tables())
    integers = (intersection, peak_offsets, node_valid)

    def swap(first):
        pairs = [(i, i + 1) for i in range(first, secs - 1, 2)]
        return pairs + [(b, a) for a, b in pairs]

    sent_far = spectra(
        features, integers, columns, rows, functools.partial(sent_place, far=True), BATCHES, 2 * NOTE, 50
    )
    got_far = lax.ppermute(sent_far, "sec", swap(1))
    sent_near = spectra(
        features, integers, columns, rows, functools.partial(sent_place, far=False), BATCHES, NOTE, 50,
        (sent_far,),
    )
    got_near = lax.ppermute(sent_near, "sec", swap(0))
    rest = spectra(
        features, integers, columns, rows, rest_place, 2 * BATCHES, 0, 44, (sent_near,)
    )

    smem = pl.BlockSpec(memory_space=pltpu.SMEM)
    vmem = pl.BlockSpec(memory_space=pltpu.VMEM)
    row_shape = jax.ShapeDtypeStruct((1, LANES), jnp.float32)

    def call(kernel, in_specs, out_shape, pairs, *args):
        lead = (2,) if pairs == 2 else ()
        return pl.pallas_call(
            kernel,
            in_specs=in_specs,
            out_specs=vmem,
            out_shape=out_shape,
            scratch_shapes=[
                pltpu.VMEM(lead + (2, WIDTH, LANES), jnp.float32),
                pltpu.VMEM(lead + (2, 8, LANES), jnp.float32),
            ],
            compiler_params=pltpu.CompilerParams(vmem_limit_bytes=16 * 1024 * 1024),
            cost_estimate=pl.CostEstimate(
                flops=1, bytes_accessed=1, transcendentals=0
            ),
        )(*args)

    phases = (row_phase, unit_phase, col_phase)
    local = call(
        local_kernel, [smem] * 3 + [vmem] * 6, row_shape, 2, *integers, sent_far, sent_near, rest, *phases
    )
    near = call(
        functools.partial(met_kernel, far=False), [smem] * 3 + [vmem] * 6, row_shape, 1,
        *integers, rest, got_near, *phases, local,
    )
    message = call(
        functools.partial(met_kernel, far=True), [smem] * 3 + [vmem] * 6,
        jax.ShapeDtypeStruct((secs * strips, 1, LANES), jnp.float32), 1,
        *integers, rest, got_far, *phases, near,
    )

    gathered = lax.all_to_all(message, ("strip", "sec"), 0, 0).reshape(strips, secs, LANES)
    if secs < 64:
        gathered = jnp.pad(gathered, ((0, 0), (0, 64 - secs), (0, 0)))
    gathered = gathered.reshape(strips * 64, LANES)
    scores, positions = pl.pallas_call(
        relax_kernel,
        in_specs=[vmem],
        out_specs=[vmem, vmem],
        out_shape=[
            jax.ShapeDtypeStruct((2, 2, 5), jnp.float32),
            jax.ShapeDtypeStruct((2, 2, 2), jnp.float32),
        ],
        scratch_shapes=[pltpu.VMEM((2, 8, LANES), jnp.float32)],
        compiler_params=pltpu.CompilerParams(vmem_limit_bytes=4 * 1024 * 1024),
    )(gathered)
    return scores, positions


def solution(mesh):
    placed = (
        P("sec", "strip", None, None, None),
        P("sec", "strip", None),
        P("sec", "strip", None),
        P("sec", "strip"),
    )
    return jax.shard_map(
        body,
        mesh=mesh,
        in_specs=placed,
        out_specs=(P("sec", "strip", None), P("sec", "strip", None)),
        check_vma=False,
    )
```

```python
import functools
import math

import jax
import jax.numpy as jnp
import ml_dtypes
import numpy as np
from jax import lax
from jax.experimental import pallas as pl
from jax.experimental.pallas import tpu as pltpu
from jax.sharding import PartitionSpec as P

ITERS = 8
KAPPA = 1.0
STEP_SIZE = 0.2
UNIT_SCALE = 0.125

WIDTH = 160
HALF = 80
LANES = 128
BATCH = 8
GROUPS = 5
PACKED = GROUPS * LANES
CHANNELS = 32
BATCHES = CHANNELS // BATCH
REACH = 13
BLOCK = 2 * WIDTH
CROSS_UNROLL = 10
SCORES = 72
PER_STEP = 2
NOTE = 16

SHIFTS = [(HALF * i) % LANES for i in range(BATCH)]
PIECES = [
    [(80, 0), (128, 1)],
    [(32, 1), (112, 2), (128, 3)],
    [(64, 3), (128, 4)],
    [(16, 4), (96, 5), (128, 6)],
    [(48, 6), (128, 7)],
]
STARTS = [[0, 80], [32, 112], [64], [16, 96], [48]]
ROW_FREQ = np.concatenate([np.arange(HALF), [HALF], -np.arange(1, HALF)])


def angle(product):
    return 2.0 * math.pi / WIDTH * (product % WIDTH)


def tables():
    counter = np.arange(WIDTH)
    angles = angle(counter[:, None] * counter[None, :])
    cosine, sine = np.cos(angles), np.sin(angles)
    cos_part = cosine[:HALF]
    sin_part = np.concatenate([cosine[HALF : HALF + 1], sine[1:HALF]], axis=0)
    rows = np.concatenate([cos_part, sin_part], axis=0)
    columns = np.zeros((WIDTH, 2 * LANES))
    columns[:, :HALF] = cos_part.T
    columns[:, LANES : LANES + HALF] = sin_part.T
    return columns.astype(ml_dtypes.bfloat16), rows.astype(ml_dtypes.bfloat16)


def phase_tables():
    peaks = np.arange(-REACH, REACH + 1)
    rows = np.zeros((WIDTH, LANES))
    a = angle(ROW_FREQ[:, None] * peaks[None, :])
    rows[:, : len(peaks)] = np.cos(a)
    rows[:, 64 : 64 + len(peaks)] = np.sin(a)
    unit = np.zeros((2, WIDTH, LANES))
    unit[0] = np.cos(angle(ROW_FREQ))[:, None]
    unit[1] = np.sin(angle(ROW_FREQ))[:, None]
    columns = np.zeros((4, 32, LANES))
    low = np.arange(HALF)
    high = low.copy()
    high[0] = HALF
    for h, freq in enumerate((low, high)):
        b = angle(peaks[:, None] * freq[None, :])
        columns[2 * h, : len(peaks), :HALF] = np.cos(b)
        columns[2 * h + 1, : len(peaks), :HALF] = np.sin(b)
    return rows.astype(np.float32), unit.astype(np.float32), columns.astype(np.float32)


def transform(image, columns_ref, rows_ref, packed_ref, store):
    lane2 = lax.broadcasted_iota(jnp.int32, (1, 2 * LANES), 1) % LANES
    halves = {}

    def half(i):
        halves[i] = jnp.dot(image(i), columns_ref[i], preferred_element_type=jnp.float32)

    def pack(group):
        pieces = PIECES[group]
        value = halves[pieces[-1][1]]
        for end, i in pieces[-2::-1]:
            value = jnp.where(lane2 < end, halves[i], value)
        packed_ref[:, group * 2 * LANES : (group + 1) * 2 * LANES] = value.astype(jnp.bfloat16)

    lane = lax.broadcasted_iota(jnp.int32, (1, LANES), 1)
    edge = lax.broadcasted_iota(jnp.int32, (16, LANES), 0) == 0

    def finish(group):
        whole = jnp.dot(
            rows_ref[...],
            packed_ref[:, group * 2 * LANES : (group + 1) * 2 * LANES],
            preferred_element_type=jnp.float32,
        )
        first = lane == STARTS[group][0]
        for start in STARTS[group][1:]:
            first = first | (lane == start)
        cc, cs = whole[:HALF, :LANES], whole[:HALF, LANES:]
        sc, ss = whole[HALF:, :LANES], whole[HALF:, LANES:]
        ss0 = jnp.where(first, 0.0, ss)
        cs0 = jnp.where(first, 0.0, cs)
        values = [
            (0, 0, cc - ss0, cc),
            (0, 1, jnp.where(first, cs, cc + ss0), jnp.where(first, cs, sc)),
            (1, 0, -(cs0 + sc), jnp.where(first, -sc, -cs)),
            (1, 1, jnp.where(first, ss, sc - cs0), jnp.where(first, ss, -ss)),
        ]
        for c, h, value, fixed in values:
            top = jnp.where(edge, fixed[:16], value[:16]).astype(jnp.bfloat16)
            store(c, h * HALF, 16, group, top)
            store(c, h * HALF + 16, HALF - 16, group, value[16:].astype(jnp.bfloat16))

    half(0)
    half(1)
    pack(0)
    half(2)
    half(3)
    pack(1)
    finish(0)
    half(4)
    pack(2)
    finish(1)
    half(5)
    half(6)
    pack(3)
    finish(2)
    half(7)
    pack(4)
    finish(3)
    finish(4)


def spectra_kernel(*refs, where, guess, count, noted, after):
    meet_in, peaks_in, valids_in, images_ref, columns_in, rows_in, *refs = refs
    refs = refs[1:] if after else refs
    out_ref, held_ref, packed_ref, base_ref, columns_ref, rows_ref, *refs = refs
    meet_ref, peaks_ref, valids_ref, sems, other_sems = refs

    def fetch(n):
        section, patch, batch = where(n, meet_ref)
        return pltpu.make_async_copy(
            images_ref.at[section, patch, pl.ds(batch * BATCH, BATCH)], held_ref.at[n], sems.at[n]
        )

    meet = pltpu.make_async_copy(meet_in, meet_ref, other_sems.at[0])
    meet.start()
    others = [
        pltpu.make_async_copy(columns_in, base_ref, other_sems.at[1]),
        pltpu.make_async_copy(rows_in, rows_ref, other_sems.at[2]),
    ]
    if noted:
        others.append(pltpu.make_async_copy(peaks_in, peaks_ref, other_sems.at[3]))
        others.append(pltpu.make_async_copy(valids_in, valids_ref, other_sems.at[4]))
    for other in others:
        other.start()
    guesses = [
        pltpu.make_async_copy(
            images_ref.at[section, patch, pl.ds(0, BATCH)], held_ref.at[slot], sems.at[slot]
        )
        for (section, patch), slot in zip(guess(), (0, count))
    ]
    for copy in guesses:
        copy.start()
    meet.wait()
    for n in range(1, count):
        fetch(n).start()
    for other in others:
        other.wait()
    for g in range(2):
        lanes = slice(g * LANES, (g + 1) * LANES)
        base = base_ref[:, lanes].astype(jnp.float32)
        for i, shift in enumerate(SHIFTS):
            moved = pltpu.roll(base, shift, 1) if shift else base
            columns_ref[i, :, lanes] = moved.astype(jnp.bfloat16)

    for copy in guesses:
        copy.wait()
    began = jnp.where(where(0, meet_ref)[1] == guess()[0][1], 0, count)

    def one(n, slot):
        pl.when(n > 0)(lambda: fetch(n).wait())
        at_held = jnp.where(n == 0, began, n)

        def store(c, row, size, group, value):
            at = pl.multiple_of(n * BLOCK + c * WIDTH + row, 16)
            out_ref[pl.ds(at, size), group * LANES : (group + 1) * LANES] = value

        transform(lambda i: held_ref[at_held, i], columns_ref, rows_ref, packed_ref.at[slot], store)

    def step(k, carry):
        for slot in range(PER_STEP):
            one(k * PER_STEP + slot, slot)
        return carry

    lax.fori_loop(0, count // PER_STEP, step, 0)

    if noted:
        give = 1 - meet_ref[0, 0, 0]
        lane = lax.broadcasted_iota(jnp.int32, (NOTE, PACKED), 1)
        note = jnp.zeros((NOTE, PACKED), jnp.float32)
        values = [peaks_ref[0, give, 0], peaks_ref[0, give, 1], valids_ref[0, give], give]
        for k, value in enumerate(values):
            note = jnp.where(lane == k, value.astype(jnp.float32), note)
        out_ref[count * BLOCK : count * BLOCK + NOTE, :] = note.astype(jnp.bfloat16)


def spectra(features, integers, columns, rows, where, guess, count, noted, limit, after=()):
    vmem = pl.BlockSpec(memory_space=pltpu.VMEM)
    anywhere = pl.BlockSpec(memory_space=pl.ANY)
    hbm = pl.BlockSpec(memory_space=pltpu.HBM)
    return pl.pallas_call(
        functools.partial(
            spectra_kernel, where=where, guess=guess, count=count, noted=noted, after=bool(after)
        ),
        in_specs=[hbm] * 6 + [anywhere] * len(after),
        out_specs=vmem,
        out_shape=jax.ShapeDtypeStruct((count * BLOCK + noted, PACKED), jnp.bfloat16),
        scratch_shapes=[
            pltpu.VMEM((count + 1, BATCH, WIDTH, WIDTH), jnp.bfloat16),
            pltpu.VMEM((PER_STEP, WIDTH, 2 * PACKED), jnp.bfloat16),
            pltpu.VMEM(columns.shape, jnp.bfloat16),
            pltpu.VMEM((BATCH,) + columns.shape, jnp.bfloat16),
            pltpu.VMEM(rows.shape, jnp.bfloat16),
            pltpu.SMEM(integers[0].shape, jnp.int32),
            pltpu.SMEM(integers[1].shape, jnp.int32),
            pltpu.SMEM(integers[2].shape, jnp.int32),
            pltpu.SemaphoreType.DMA((count + 1,)),
            pltpu.SemaphoreType.DMA((5,)),
        ],
        compiler_params=pltpu.CompilerParams(vmem_limit_bytes=limit * 1024 * 1024),
        cost_estimate=pl.CostEstimate(
            flops=count * BATCH * 2 * 2 * WIDTH * WIDTH,
            bytes_accessed=count * BATCH * 1400,
            transcendentals=0,
        ),
    )(*(pltpu.with_memory_space_constraint(a, pltpu.HBM) for a in (*integers, features, columns, rows)), *after)


def my_core():
    return lax.axis_index("sec") % 2


def gather_windows(g):
    lane = lax.broadcasted_iota(jnp.int32, (1, LANES), 1)
    low = lane < 80
    windows = [
        (80, jnp.where(low, g[1], g[0])),
        (32, g[1]),
        (112, jnp.where(lane < 112, g[2], g[1])),
        (64, jnp.where(lane < 64, g[3], g[2])),
        (16, g[3]),
        (96, jnp.where(lane < 96, g[4], g[3])),
        (48, g[4]),
    ]
    total = g[0]
    for shift, value in windows:
        total = total + pltpu.roll(value, LANES - shift, 1)
    return total


def cross_into(sum_ref, edge_ref, own, near, sign):
    def load(side, n, c, start, lanes):
        at = pl.multiple_of(side[1] + n * BLOCK + c * WIDTH + start, 16)
        return side[0][pl.ds(at, 16), lanes].astype(jnp.float32)

    def step(k, carry):
        start = pl.multiple_of(k * 16, 16)
        reals, imags = [], []
        for group in range(GROUPS):
            lanes = slice(group * LANES, (group + 1) * LANES)
            real = imag = None
            for n in range(BATCHES):
                own_re, own_im = (load(own, n, c, start, lanes) for c in range(2))
                near_re, near_im = (load(near, n, c, start, lanes) for c in range(2))
                re = own_re * near_re + own_im * near_im
                im = own_re * near_im - own_im * near_re
                real = re if real is None else real + re
                imag = im if imag is None else imag + im
            reals.append(real)
            imags.append(imag)
        sum_ref[0, pl.ds(start, 16), :] = gather_windows(reals)
        sum_ref[1, pl.ds(start, 16), :] = sign * gather_windows(imags)
        return carry

    lax.fori_loop(0, WIDTH // 16, step, 0, unroll=CROSS_UNROLL)
    for h in range(2):
        boths = []
        for group in range(GROUPS):
            lanes = slice(group * LANES, (group + 1) * LANES)
            both = None
            for n in range(BATCHES):
                ii = load(own, n, 1, h * HALF, lanes) * load(near, n, 1, h * HALF, lanes)
                both = ii if both is None else both + ii
            boths.append(both[:8])
        edge_ref[h] = gather_windows(boths)


def scores_of(sum_ref, edge_ref, row_ref, unit_ref, col_ref, peak_row, peak_col):
    lane = lax.broadcasted_iota(jnp.int32, (1, LANES), 1)
    damp = WIDTH * WIDTH * math.sqrt(CHANNELS)
    sums = {}
    moved = pltpu.roll(row_ref[...], (LANES - REACH) - peak_row, 1)
    for h in range(2):
        rows = slice(h * HALF, (h + 1) * HALF)
        real, imag = sum_ref[0, rows, :], sum_ref[1, rows, :]
        inverse = 1.0 / (jnp.sqrt(real * real + imag * imag) + damp)
        white_re, white_im = real * inverse, imag * inverse
        ii = edge_ref[h][0:1, :]
        rr = real[0:1, :] - ii
        z_rr = 0.5 * rr / (jnp.abs(rr) + damp)
        z_ii = 0.5 * ii / (jnp.abs(ii) + damp)
        stays, goes = (z_rr, z_ii) if h == 0 else (z_ii, z_rr)
        corner = (lax.broadcasted_iota(jnp.int32, (8, LANES), 0) == 0) & (
            lax.broadcasted_iota(jnp.int32, (8, LANES), 1) == 0
        )
        white_re = jnp.concatenate(
            [jnp.where(corner, jnp.broadcast_to(stays, (8, LANES)), white_re[:8]), white_re[8:]], 0
        )
        white_im = jnp.concatenate([jnp.where(corner, 0.0, white_im[:8]), white_im[8:]], 0)
        cos, sin = moved[rows, 0:1], moved[rows, 64:65]
        turned_re = white_re * cos - white_im * sin
        turned_im = white_re * sin + white_im * cos
        unit_cos, unit_sin = unit_ref[0, rows, :], unit_ref[1, rows, :]
        add = lambda x: jnp.sum(x, axis=0, keepdims=True)
        plain_re, plain_im = add(turned_re), add(turned_im)
        cos_re, cos_im = add(turned_re * unit_cos), add(turned_im * unit_cos)
        sin_re, sin_im = add(turned_re * unit_sin), add(turned_im * unit_sin)
        sums[h] = [
            (plain_re, plain_im),
            (cos_re + sin_im, cos_im - sin_re),
            (cos_re - sin_im, cos_im + sin_re),
        ]
        extra = jnp.where(lane == 0, goes, 0.0)
        for a in range(3):
            turn = moved[HALF : HALF + 1, 0:1] * (1.0 if a == 0 else -1.0) if h == 0 else 1.0
            sums[h][a] = (sums[h][a][0] + extra * turn, sums[h][a][1])
    out = []
    for a, b in ((0, 0), (1, 0), (2, 0), (0, -1), (0, 1)):
        total = None
        for h in range(2):
            cos = col_ref[2 * h, pl.ds(peak_col + (REACH + b), 1), :]
            sin = col_ref[2 * h + 1, pl.ds(peak_col + (REACH + b), 1), :]
            term = sums[h][a][0] * cos - sums[h][a][1] * sin
            total = term if total is None else total + term
        out.append(jnp.sum(total, axis=1, keepdims=True) * (4.0 / WIDTH))
    return out


def node_row(z, peak_row, peak_col, valid, kind, side):
    lane = lax.broadcasted_iota(jnp.int32, (1, LANES), 1)
    wide = [jnp.broadcast_to(value, (1, LANES)) for value in z]
    spread_row = jnp.abs(wide[1]) + jnp.abs(wide[0]) + jnp.abs(wide[2]) + 1.0
    spread_col = jnp.abs(wide[3]) + jnp.abs(wide[0]) + jnp.abs(wide[4]) + 1.0
    off_row = UNIT_SCALE * (
        peak_row.astype(jnp.float32) + 0.5 * (wide[2] - wide[1]) / spread_row
    )
    off_col = UNIT_SCALE * (
        peak_col.astype(jnp.float32) + 0.5 * (wide[4] - wide[3]) / spread_col
    )
    weight = valid.astype(jnp.float32) * (1.0 + jnp.tanh(wide[0]))
    first = 24 * kind + 2 * lax.axis_index("strip") + side
    row = jnp.zeros((1, LANES), jnp.float32)
    for n, value in enumerate([weight, off_row, off_col]):
        row = jnp.where(lane == first + 8 * n, value, row)
    for n, value in enumerate(wide):
        row = jnp.where(lane == SCORES + 10 * kind + 5 * side + n, value, row)
    return row


def local_kernel(
    meet_ref, peak_ref, valid_ref, far_ref, near_ref, rest_ref, row_ref, unit_ref, col_ref, out_ref,
    sum_ref, edge_ref,
):
    rest = BATCHES * BLOCK
    core = my_core()
    same = meet_ref[1, 0, 0] == 1 - meet_ref[0, 0, 0]

    @pl.when(same)
    def _():
        sign = jnp.where(core == 1, 1.0, -1.0)
        cross_into(sum_ref.at[0], edge_ref.at[0], (far_ref, 0), (near_ref, 0), sign)
        cross_into(sum_ref.at[1], edge_ref.at[1], (rest_ref, rest), (rest_ref, 0), 1.0)

    def apart(patch_ref, given_ref):
        cross_into(sum_ref.at[0], edge_ref.at[0], (patch_ref, 0), (rest_ref, 0), 1.0)
        cross_into(sum_ref.at[1], edge_ref.at[1], (rest_ref, rest), (given_ref, 0), 1.0)

    pl.when(jnp.logical_not(same) & (core == 1))(lambda: apart(far_ref, near_ref))
    pl.when(jnp.logical_not(same) & (core == 0))(lambda: apart(near_ref, far_ref))

    total = jnp.zeros((1, LANES), jnp.float32)
    for n in range(2):
        peak = peak_ref[1, n, 0], peak_ref[1, n, 1]
        z = scores_of(sum_ref.at[n], edge_ref.at[n], row_ref, unit_ref, col_ref, *peak)
        total = total + node_row(z, *peak, valid_ref[1, n], 1, n)
    out_ref[...] = total


def met_kernel(
    meet_ref, peak_ref, valid_ref, rest_ref, got_ref, row_ref, unit_ref, col_ref, before_ref,
    out_ref, sum_ref, edge_ref, *, far,
):
    after = my_core() == (1 if far else 0)
    keep = meet_ref[0, 0, 0]
    note = got_ref[BATCHES * BLOCK : BATCHES * BLOCK + NOTE, :LANES].astype(jnp.float32)[0:1, :]
    lane = lax.broadcasted_iota(jnp.int32, (1, LANES), 1)
    held = [jnp.sum(jnp.where(lane == k, note, 0.0)).astype(jnp.int32) for k in range(4)]
    peak_row = jnp.where(after, held[0], peak_ref[0, keep, 0])
    peak_col = jnp.where(after, held[1], peak_ref[0, keep, 1])
    valid = jnp.where(after, held[2], valid_ref[0, keep])
    kind = jnp.where(after, 2, 0)
    side = jnp.where(after, held[3], keep)
    start = jnp.where(after, BATCHES * BLOCK, 0)
    sign = jnp.where(after, -1.0, 1.0)
    cross_into(sum_ref, edge_ref, (rest_ref, start), (got_ref, 0), sign)
    z = scores_of(sum_ref, edge_ref, row_ref, unit_ref, col_ref, peak_row, peak_col)
    total = before_ref[...] + node_row(z, peak_row, peak_col, valid, kind, side)
    out_ref[...] = jnp.broadcast_to(total, (1, LANES)) if not far else jnp.broadcast_to(
        total[None], out_ref.shape
    )


def relax_kernel(all_ref, scores_ref, positions_ref, hold_ref):
    sec, strip = lax.axis_index("sec"), lax.axis_index("strip")
    strips = 4
    lane = lax.broadcasted_iota(jnp.int32, (8, LANES), 1)
    row = lax.broadcasted_iota(jnp.int32, (8, LANES), 0)
    seat = lane % 64
    blocks = [all_ref[t * 64 : (t + 1) * 64, :] for t in range(strips)]
    joined = (blocks[0] + blocks[1]) + (blocks[2] + blocks[3])
    turned = jnp.concatenate([joined, jnp.zeros((64, LANES), jnp.float32)], axis=0).T

    def field(n):
        return turned[8 * n : 8 * n + 8]

    def both(low, high):
        return jnp.where(lane < 64, low, pltpu.roll(high, 64, 1))

    def first(n):
        return field(n) + jnp.where(lane == 0, 0.0, pltpu.roll(field(6 + n), 1, 1))

    w_a = jnp.where(lane == 0, 0.0, first(0))
    w_a, w_b = both(w_a, w_a), both(field(3), field(3))
    o_a = both(first(1), first(2))
    o_b = both(field(4), field(5))
    drift_a = jnp.sum(w_a * o_a, axis=0, keepdims=True) / (
        jnp.sum(w_a, axis=0, keepdims=True) + 1.0
    )
    drift_b = jnp.sum(w_b * o_b, axis=0, keepdims=True) / (
        jnp.sum(w_b, axis=0, keepdims=True) + 1.0
    )
    drift_a = jnp.broadcast_to(drift_a, (8, LANES))
    drift_b = jnp.broadcast_to(drift_b, (8, LANES))
    run = drift_a + drift_b
    for shift in (1, 2, 4, 8, 16, 32):
        run = run + jnp.where(seat >= shift, pltpu.roll(run, shift, 1), 0.0)
    p_b = run
    p_a = run - drift_b

    def links(p):
        left = jnp.where(row > 0, pltpu.roll(p, 1, 0), p)
        right = jnp.where(row < 7, pltpu.roll(p, 7, 0), p)
        return (p - left) + (p - right)

    w_next = pltpu.roll(w_a, LANES - 1, 1)
    o_next = pltpu.roll(o_a, LANES - 1, 1)
    for _ in range(ITERS):
        before = pltpu.roll(p_b, 1, 1)
        after = pltpu.roll(p_a, LANES - 1, 1)
        e_a = w_a * (p_a - before - o_a)
        e_b = w_b * (p_b - p_a - o_b)
        e_next = w_next * (after - p_b - o_next)
        n_a = p_a - STEP_SIZE * (e_a - e_b + KAPPA * links(p_a))
        n_b = p_b - STEP_SIZE * (e_b - e_next + KAPPA * links(p_b))
        p_a, p_b = n_a, n_b
    for s, p in enumerate((p_a, p_b)):
        first = jnp.sum(jnp.where(lane == sec, p, 0.0), axis=1, keepdims=True)
        other = jnp.sum(jnp.where(lane == sec + 64, p, 0.0), axis=1, keepdims=True)
        hold_ref[s] = jnp.where(lane == 0, first, other)
        for i in range(2):
            positions_ref[s, i : i + 1, :] = hold_ref[s, pl.ds(2 * strip + i, 1), :][:, :2]
    own = all_ref[pl.ds(strip * 64 + sec, 1), :]
    earlier = all_ref[pl.ds(strip * 64 + jnp.maximum(sec - 1, 0), 1), :]
    earlier = jnp.where(sec > 0, earlier, 0.0)
    for i in range(2):
        shift = LANES - SCORES - 5 * i
        value = pltpu.roll(own, shift, 1) + pltpu.roll(earlier, shift - 20, 1)
        scores_ref[0, i : i + 1, :] = value[:, :5]
        scores_ref[1, i : i + 1, :] = pltpu.roll(own, shift - 10, 1)[:, :5]


def sent_place(n, meet_ref, far):
    up = (my_core() == 1) == far
    return jnp.where(up, 1, 0), jnp.where(up, 0, 1 - meet_ref[0, 0, 0]), n


def sent_guess(far):
    up = (my_core() == 1) == far
    return (jnp.where(up, 1, 0), 0), (0, 1)


def rest_guess():
    return (0, 0), (0, 1)


def rest_place(n, meet_ref):
    late = n // BATCHES
    return late, jnp.where(late == 0, meet_ref[0, 0, 0], 1), n % BATCHES


def body(features, intersection, peak_offsets, node_valid):
    secs, strips = lax.axis_size("sec"), lax.axis_size("strip")
    columns, rows = (jnp.asarray(t) for t in tables())
    row_phase, unit_phase, col_phase = (jnp.asarray(t) for t in phase_tables())
    integers = (intersection, peak_offsets, node_valid)

    def swap(first):
        pairs = [(i, i + 1) for i in range(first, secs - 1, 2)]
        return pairs + [(b, a) for a, b in pairs]

    sent_far = spectra(
        features, integers, columns, rows, functools.partial(sent_place, far=True),
        functools.partial(sent_guess, far=True), BATCHES, 2 * NOTE, 50,
    )
    got_far = lax.ppermute(sent_far, "sec", swap(1))
    sent_near = spectra(
        features, integers, columns, rows, functools.partial(sent_place, far=False),
        functools.partial(sent_guess, far=False), BATCHES, NOTE, 50,
        (sent_far,),
    )
    got_near = lax.ppermute(sent_near, "sec", swap(0))
    rest = spectra(
        features, integers, columns, rows, rest_place, rest_guess, 2 * BATCHES, 0, 44, (sent_near,)
    )

    smem = pl.BlockSpec(memory_space=pltpu.SMEM)
    vmem = pl.BlockSpec(memory_space=pltpu.VMEM)
    row_shape = jax.ShapeDtypeStruct((1, LANES), jnp.float32)

    def call(kernel, in_specs, out_shape, pairs, *args):
        lead = (2,) if pairs == 2 else ()
        return pl.pallas_call(
            kernel,
            in_specs=in_specs,
            out_specs=vmem,
            out_shape=out_shape,
            scratch_shapes=[
                pltpu.VMEM(lead + (2, WIDTH, LANES), jnp.float32),
                pltpu.VMEM(lead + (2, 8, LANES), jnp.float32),
            ],
            compiler_params=pltpu.CompilerParams(vmem_limit_bytes=16 * 1024 * 1024),
            cost_estimate=pl.CostEstimate(
                flops=1, bytes_accessed=1, transcendentals=0
            ),
        )(*args)

    phases = (row_phase, unit_phase, col_phase)
    local = call(
        local_kernel, [smem] * 3 + [vmem] * 6, row_shape, 2, *integers, sent_far, sent_near, rest, *phases
    )
    near = call(
        functools.partial(met_kernel, far=False), [smem] * 3 + [vmem] * 6, row_shape, 1,
        *integers, rest, got_near, *phases, local,
    )
    message = call(
        functools.partial(met_kernel, far=True), [smem] * 3 + [vmem] * 6,
        jax.ShapeDtypeStruct((secs * strips, 1, LANES), jnp.float32), 1,
        *integers, rest, got_far, *phases, near,
    )

    gathered = lax.all_to_all(message, ("strip", "sec"), 0, 0).reshape(strips, secs, LANES)
    if secs < 64:
        gathered = jnp.pad(gathered, ((0, 0), (0, 64 - secs), (0, 0)))
    gathered = gathered.reshape(strips * 64, LANES)
    scores, positions = pl.pallas_call(
        relax_kernel,
        in_specs=[vmem],
        out_specs=[vmem, vmem],
        out_shape=[
            jax.ShapeDtypeStruct((2, 2, 5), jnp.float32),
            jax.ShapeDtypeStruct((2, 2, 2), jnp.float32),
        ],
        scratch_shapes=[pltpu.VMEM((2, 8, LANES), jnp.float32)],
        compiler_params=pltpu.CompilerParams(vmem_limit_bytes=4 * 1024 * 1024),
    )(gathered)
    return scores, positions


def solution(mesh):
    placed = (
        P("sec", "strip", None, None, None),
        P("sec", "strip", None),
        P("sec", "strip", None),
        P("sec", "strip"),
    )
    return jax.shard_map(
        body,
        mesh=mesh,
        in_specs=placed,
        out_specs=(P("sec", "strip", None), P("sec", "strip", None)),
        check_vma=False,
    )
```

```python
import functools
import math

import jax
import jax.numpy as jnp
import ml_dtypes
import numpy as np
from jax import lax
from jax.experimental import pallas as pl
from jax.experimental.pallas import tpu as pltpu
from jax.sharding import PartitionSpec as P

ITERS = 8
KAPPA = 1.0
STEP_SIZE = 0.2
UNIT_SCALE = 0.125

WIDTH = 160
HALF = 80
LANES = 128
BATCH = 8
GROUPS = 5
PACKED = GROUPS * LANES
CHANNELS = 32
BATCHES = CHANNELS // BATCH
REACH = 13
BLOCK = 2 * WIDTH
CROSS_UNROLL = 10
SCORES = 72
PER_STEP = 2
FAR = (2, 2)
NEAR = (1, 1, 2)
SPARE = (2, 1)
NOTE = 16

SHIFTS = [(HALF * i) % LANES for i in range(BATCH)]
PIECES = [
    [(80, 0), (128, 1)],
    [(32, 1), (112, 2), (128, 3)],
    [(64, 3), (128, 4)],
    [(16, 4), (96, 5), (128, 6)],
    [(48, 6), (128, 7)],
]
STARTS = [[0, 80], [32, 112], [64], [16, 96], [48]]
ROW_FREQ = np.concatenate([np.arange(HALF), [HALF], -np.arange(1, HALF)])


def angle(product):
    return 2.0 * math.pi / WIDTH * (product % WIDTH)


def tables():
    counter = np.arange(WIDTH)
    angles = angle(counter[:, None] * counter[None, :])
    cosine, sine = np.cos(angles), np.sin(angles)
    cos_part = cosine[:HALF]
    sin_part = np.concatenate([cosine[HALF : HALF + 1], sine[1:HALF]], axis=0)
    rows = np.concatenate([cos_part, sin_part], axis=0)
    columns = np.zeros((WIDTH, 2 * LANES))
    columns[:, :HALF] = cos_part.T
    columns[:, LANES : LANES + HALF] = sin_part.T
    return columns.astype(ml_dtypes.bfloat16), rows.astype(ml_dtypes.bfloat16)


def phase_tables():
    peaks = np.arange(-REACH, REACH + 1)
    rows = np.zeros((WIDTH, LANES))
    a = angle(ROW_FREQ[:, None] * peaks[None, :])
    rows[:, : len(peaks)] = np.cos(a)
    rows[:, 64 : 64 + len(peaks)] = np.sin(a)
    unit = np.zeros((2, WIDTH, LANES))
    unit[0] = np.cos(angle(ROW_FREQ))[:, None]
    unit[1] = np.sin(angle(ROW_FREQ))[:, None]
    columns = np.zeros((4, 32, LANES))
    low = np.arange(HALF)
    high = low.copy()
    high[0] = HALF
    for h, freq in enumerate((low, high)):
        b = angle(peaks[:, None] * freq[None, :])
        columns[2 * h, : len(peaks), :HALF] = np.cos(b)
        columns[2 * h + 1, : len(peaks), :HALF] = np.sin(b)
    return rows.astype(np.float32), unit.astype(np.float32), columns.astype(np.float32)


def transform(image, columns_ref, rows_ref, packed_ref, store):
    lane2 = lax.broadcasted_iota(jnp.int32, (1, 2 * LANES), 1) % LANES
    halves = {}

    def half(i):
        halves[i] = jnp.dot(image(i), columns_ref[i], preferred_element_type=jnp.float32)

    def pack(group):
        pieces = PIECES[group]
        value = halves[pieces[-1][1]]
        for end, i in pieces[-2::-1]:
            value = jnp.where(lane2 < end, halves[i], value)
        packed_ref[:, group * 2 * LANES : (group + 1) * 2 * LANES] = value.astype(jnp.bfloat16)

    lane = lax.broadcasted_iota(jnp.int32, (1, LANES), 1)
    edge = lax.broadcasted_iota(jnp.int32, (16, LANES), 0) == 0

    def finish(group):
        whole = jnp.dot(
            rows_ref[...],
            packed_ref[:, group * 2 * LANES : (group + 1) * 2 * LANES],
            preferred_element_type=jnp.float32,
        )
        first = lane == STARTS[group][0]
        for start in STARTS[group][1:]:
            first = first | (lane == start)
        cc, cs = whole[:HALF, :LANES], whole[:HALF, LANES:]
        sc, ss = whole[HALF:, :LANES], whole[HALF:, LANES:]
        ss0 = jnp.where(first, 0.0, ss)
        cs0 = jnp.where(first, 0.0, cs)
        values = [
            (0, 0, cc - ss0, cc),
            (0, 1, jnp.where(first, cs, cc + ss0), jnp.where(first, cs, sc)),
            (1, 0, -(cs0 + sc), jnp.where(first, -sc, -cs)),
            (1, 1, jnp.where(first, ss, sc - cs0), jnp.where(first, ss, -ss)),
        ]
        for c, h, value, fixed in values:
            top = jnp.where(edge, fixed[:16], value[:16]).astype(jnp.bfloat16)
            store(c, h * HALF, 16, group, top)
            store(c, h * HALF + 16, HALF - 16, group, value[16:].astype(jnp.bfloat16))

    half(0)
    half(1)
    pack(0)
    half(2)
    half(3)
    pack(1)
    finish(0)
    half(4)
    pack(2)
    finish(1)
    half(5)
    half(6)
    pack(3)
    finish(2)
    half(7)
    pack(4)
    finish(3)
    finish(4)


def spectra_kernel(*refs, where, guess, begin, parts, noted, after):
    count = sum(parts)
    meet_in, peaks_in, valids_in, images_ref, columns_in, rows_in, *refs = refs
    refs = refs[1:] if after else refs
    outs, refs = refs[: len(parts)], refs[len(parts) :]
    held_ref, packed_ref, base_ref, columns_ref, rows_ref, *refs = refs
    meet_ref, peaks_ref, valids_ref, sems, other_sems = refs

    def fetch(n):
        section, patch, batch = where(n, meet_ref)
        return pltpu.make_async_copy(
            images_ref.at[section, patch, pl.ds(batch * BATCH, BATCH)], held_ref.at[n], sems.at[n]
        )

    meet = pltpu.make_async_copy(meet_in, meet_ref, other_sems.at[0])
    meet.start()
    others = [
        pltpu.make_async_copy(columns_in, base_ref, other_sems.at[1]),
        pltpu.make_async_copy(rows_in, rows_ref, other_sems.at[2]),
    ]
    if noted is not None:
        others.append(pltpu.make_async_copy(peaks_in, peaks_ref, other_sems.at[3]))
        others.append(pltpu.make_async_copy(valids_in, valids_ref, other_sems.at[4]))
    for other in others:
        other.start()
    guesses = [
        pltpu.make_async_copy(
            images_ref.at[section, patch, pl.ds(begin * BATCH, BATCH)], held_ref.at[slot], sems.at[slot]
        )
        for (section, patch), slot in zip(guess(), (0, count))
    ]
    for copy in guesses:
        copy.start()
    meet.wait()
    for n in range(1, count):
        fetch(n).start()
    for other in others:
        other.wait()
    for g in range(2):
        lanes = slice(g * LANES, (g + 1) * LANES)
        base = base_ref[:, lanes].astype(jnp.float32)
        for i, shift in enumerate(SHIFTS):
            moved = pltpu.roll(base, shift, 1) if shift else base
            columns_ref[i, :, lanes] = moved.astype(jnp.bfloat16)

    for copy in guesses:
        copy.wait()
    began = jnp.where(where(0, meet_ref)[1] == guess()[0][1], 0, count)

    def one(n, slot, out_ref, base):
        static = isinstance(n, int)
        if static and n > 0:
            fetch(n).wait()
        elif not static:
            pl.when(n > 0)(lambda: fetch(n).wait())
        at_held = jnp.where(n == 0, began, n)

        def store(c, row, size, group, value):
            at = pl.multiple_of(base + c * WIDTH + row, 16)
            out_ref[pl.ds(at, size), group * LANES : (group + 1) * LANES] = value

        transform(lambda i: held_ref[at_held, i], columns_ref, rows_ref, packed_ref.at[slot], store)

    first = 0
    for out_ref, size in zip(outs, parts):
        if size <= PER_STEP:
            for n in range(size):
                one(first + n, (first + n) % PER_STEP, out_ref, n * BLOCK)
        else:

            def step(k, carry, out_ref=out_ref, first=first):
                for slot in range(PER_STEP):
                    n = k * PER_STEP + slot
                    one(first + n, slot, out_ref, n * BLOCK)
                return carry

            lax.fori_loop(0, size // PER_STEP, step, 0)
        first += size

    if noted is not None:
        give = 1 - meet_ref[0, 0, 0]
        lane = lax.broadcasted_iota(jnp.int32, (NOTE, PACKED), 1)
        note = jnp.zeros((NOTE, PACKED), jnp.float32)
        values = [peaks_ref[0, give, 0], peaks_ref[0, give, 1], valids_ref[0, give], give]
        for k, value in enumerate(values):
            note = jnp.where(lane == k, value.astype(jnp.float32), note)
        behind = parts[noted] * BLOCK
        outs[noted][behind : behind + NOTE, :] = note.astype(jnp.bfloat16)


def spectra(features, integers, columns, rows, where, guess, begin, parts, spare, noted, limit, after=()):
    count = sum(parts)
    vmem = pl.BlockSpec(memory_space=pltpu.VMEM)
    anywhere = pl.BlockSpec(memory_space=pl.ANY)
    hbm = pl.BlockSpec(memory_space=pltpu.HBM)
    return pl.pallas_call(
        functools.partial(
            spectra_kernel, where=where, guess=guess, begin=begin, parts=parts, noted=noted,
            after=bool(after),
        ),
        in_specs=[hbm] * 6 + [anywhere] * len(after),
        out_specs=[vmem] * len(parts),
        out_shape=[
            jax.ShapeDtypeStruct((n * BLOCK + NOTE * k, PACKED), jnp.bfloat16)
            for n, k in zip(parts, spare)
        ],
        scratch_shapes=[
            pltpu.VMEM((count + 1, BATCH, WIDTH, WIDTH), jnp.bfloat16),
            pltpu.VMEM((PER_STEP, WIDTH, 2 * PACKED), jnp.bfloat16),
            pltpu.VMEM(columns.shape, jnp.bfloat16),
            pltpu.VMEM((BATCH,) + columns.shape, jnp.bfloat16),
            pltpu.VMEM(rows.shape, jnp.bfloat16),
            pltpu.SMEM(integers[0].shape, jnp.int32),
            pltpu.SMEM(integers[1].shape, jnp.int32),
            pltpu.SMEM(integers[2].shape, jnp.int32),
            pltpu.SemaphoreType.DMA((count + 1,)),
            pltpu.SemaphoreType.DMA((5,)),
        ],
        compiler_params=pltpu.CompilerParams(vmem_limit_bytes=limit * 1024 * 1024),
        cost_estimate=pl.CostEstimate(
            flops=count * BATCH * 2 * 2 * WIDTH * WIDTH,
            bytes_accessed=count * BATCH * 1400,
            transcendentals=0,
        ),
    )(*(pltpu.with_memory_space_constraint(a, pltpu.HBM) for a in (*integers, features, columns, rows)), *after)


def my_core():
    return lax.axis_index("sec") % 2


def gather_windows(g):
    lane = lax.broadcasted_iota(jnp.int32, (1, LANES), 1)
    low = lane < 80
    windows = [
        (80, jnp.where(low, g[1], g[0])),
        (32, g[1]),
        (112, jnp.where(lane < 112, g[2], g[1])),
        (64, jnp.where(lane < 64, g[3], g[2])),
        (16, g[3]),
        (96, jnp.where(lane < 96, g[4], g[3])),
        (48, g[4]),
    ]
    total = g[0]
    for shift, value in windows:
        total = total + pltpu.roll(value, LANES - shift, 1)
    return total


def cross_into(sum_ref, edge_ref, own, near, sign):
    def load(side, n, c, start, lanes):
        ref, base = side[n]
        at = pl.multiple_of(base + c * WIDTH + start, 16)
        return ref[pl.ds(at, 16), lanes].astype(jnp.float32)

    def step(k, carry):
        start = pl.multiple_of(k * 16, 16)
        reals, imags = [], []
        for group in range(GROUPS):
            lanes = slice(group * LANES, (group + 1) * LANES)
            real = imag = None
            for n in range(BATCHES):
                own_re, own_im = (load(own, n, c, start, lanes) for c in range(2))
                near_re, near_im = (load(near, n, c, start, lanes) for c in range(2))
                re = own_re * near_re + own_im * near_im
                im = own_re * near_im - own_im * near_re
                real = re if real is None else real + re
                imag = im if imag is None else imag + im
            reals.append(real)
            imags.append(imag)
        sum_ref[0, pl.ds(start, 16), :] = gather_windows(reals)
        sum_ref[1, pl.ds(start, 16), :] = sign * gather_windows(imags)
        return carry

    lax.fori_loop(0, WIDTH // 16, step, 0, unroll=CROSS_UNROLL)
    for h in range(2):
        boths = []
        for group in range(GROUPS):
            lanes = slice(group * LANES, (group + 1) * LANES)
            both = None
            for n in range(BATCHES):
                ii = load(own, n, 1, h * HALF, lanes) * load(near, n, 1, h * HALF, lanes)
                both = ii if both is None else both + ii
            boths.append(both[:8])
        edge_ref[h] = gather_windows(boths)


def scores_of(sum_ref, edge_ref, row_ref, unit_ref, col_ref, peak_row, peak_col):
    lane = lax.broadcasted_iota(jnp.int32, (1, LANES), 1)
    damp = WIDTH * WIDTH * math.sqrt(CHANNELS)
    sums = {}
    moved = pltpu.roll(row_ref[...], (LANES - REACH) - peak_row, 1)
    for h in range(2):
        rows = slice(h * HALF, (h + 1) * HALF)
        real, imag = sum_ref[0, rows, :], sum_ref[1, rows, :]
        inverse = 1.0 / (jnp.sqrt(real * real + imag * imag) + damp)
        white_re, white_im = real * inverse, imag * inverse
        ii = edge_ref[h][0:1, :]
        rr = real[0:1, :] - ii
        z_rr = 0.5 * rr / (jnp.abs(rr) + damp)
        z_ii = 0.5 * ii / (jnp.abs(ii) + damp)
        stays, goes = (z_rr, z_ii) if h == 0 else (z_ii, z_rr)
        corner = (lax.broadcasted_iota(jnp.int32, (8, LANES), 0) == 0) & (
            lax.broadcasted_iota(jnp.int32, (8, LANES), 1) == 0
        )
        white_re = jnp.concatenate(
            [jnp.where(corner, jnp.broadcast_to(stays, (8, LANES)), white_re[:8]), white_re[8:]], 0
        )
        white_im = jnp.concatenate([jnp.where(corner, 0.0, white_im[:8]), white_im[8:]], 0)
        cos, sin = moved[rows, 0:1], moved[rows, 64:65]
        turned_re = white_re * cos - white_im * sin
        turned_im = white_re * sin + white_im * cos
        unit_cos, unit_sin = unit_ref[0, rows, :], unit_ref[1, rows, :]
        add = lambda x: jnp.sum(x, axis=0, keepdims=True)
        plain_re, plain_im = add(turned_re), add(turned_im)
        cos_re, cos_im = add(turned_re * unit_cos), add(turned_im * unit_cos)
        sin_re, sin_im = add(turned_re * unit_sin), add(turned_im * unit_sin)
        sums[h] = [
            (plain_re, plain_im),
            (cos_re + sin_im, cos_im - sin_re),
            (cos_re - sin_im, cos_im + sin_re),
        ]
        extra = jnp.where(lane == 0, goes, 0.0)
        for a in range(3):
            turn = moved[HALF : HALF + 1, 0:1] * (1.0 if a == 0 else -1.0) if h == 0 else 1.0
            sums[h][a] = (sums[h][a][0] + extra * turn, sums[h][a][1])
    out = []
    for a, b in ((0, 0), (1, 0), (2, 0), (0, -1), (0, 1)):
        total = None
        for h in range(2):
            cos = col_ref[2 * h, pl.ds(peak_col + (REACH + b), 1), :]
            sin = col_ref[2 * h + 1, pl.ds(peak_col + (REACH + b), 1), :]
            term = sums[h][a][0] * cos - sums[h][a][1] * sin
            total = term if total is None else total + term
        out.append(jnp.sum(total, axis=1, keepdims=True) * (4.0 / WIDTH))
    return out


def node_row(z, peak_row, peak_col, valid, kind, side):
    lane = lax.broadcasted_iota(jnp.int32, (1, LANES), 1)
    wide = [jnp.broadcast_to(value, (1, LANES)) for value in z]
    spread_row = jnp.abs(wide[1]) + jnp.abs(wide[0]) + jnp.abs(wide[2]) + 1.0
    spread_col = jnp.abs(wide[3]) + jnp.abs(wide[0]) + jnp.abs(wide[4]) + 1.0
    off_row = UNIT_SCALE * (
        peak_row.astype(jnp.float32) + 0.5 * (wide[2] - wide[1]) / spread_row
    )
    off_col = UNIT_SCALE * (
        peak_col.astype(jnp.float32) + 0.5 * (wide[4] - wide[3]) / spread_col
    )
    weight = valid.astype(jnp.float32) * (1.0 + jnp.tanh(wide[0]))
    first = 24 * kind + 2 * lax.axis_index("strip") + side
    row = jnp.zeros((1, LANES), jnp.float32)
    for n, value in enumerate([weight, off_row, off_col]):
        row = jnp.where(lane == first + 8 * n, value, row)
    for n, value in enumerate(wide):
        row = jnp.where(lane == SCORES + 10 * kind + 5 * side + n, value, row)
    return row


def batches_of(refs, shares, start=0):
    return [(ref, start + n * BLOCK) for ref, share in zip(refs, shares) for n in range(share)]


def local_kernel(meet_ref, peak_ref, valid_ref, *refs):
    far = batches_of(refs[: len(FAR)], FAR)
    near = batches_of(refs[len(FAR) : len(FAR) + len(NEAR)], NEAR)
    rest_ref, row_ref, unit_ref, col_ref, out_ref, sum_ref, edge_ref = refs[len(FAR) + len(NEAR) :]
    first = batches_of([rest_ref], [BATCHES])
    second = batches_of([rest_ref], [BATCHES], BATCHES * BLOCK)
    core = my_core()
    same = meet_ref[1, 0, 0] == 1 - meet_ref[0, 0, 0]

    @pl.when(same)
    def _():
        sign = jnp.where(core == 1, 1.0, -1.0)
        cross_into(sum_ref.at[0], edge_ref.at[0], far, near, sign)
        cross_into(sum_ref.at[1], edge_ref.at[1], second, first, 1.0)

    def apart(patch, given):
        cross_into(sum_ref.at[0], edge_ref.at[0], patch, first, 1.0)
        cross_into(sum_ref.at[1], edge_ref.at[1], second, given, 1.0)

    pl.when(jnp.logical_not(same) & (core == 1))(lambda: apart(far, near))
    pl.when(jnp.logical_not(same) & (core == 0))(lambda: apart(near, far))

    total = jnp.zeros((1, LANES), jnp.float32)
    for n in range(2):
        peak = peak_ref[1, n, 0], peak_ref[1, n, 1]
        z = scores_of(sum_ref.at[n], edge_ref.at[n], row_ref, unit_ref, col_ref, *peak)
        total = total + node_row(z, *peak, valid_ref[1, n], 1, n)
    out_ref[...] = total


def met_kernel(meet_ref, peak_ref, valid_ref, rest_ref, *refs, far):
    shares = FAR if far else NEAR
    got, refs = refs[: len(shares)], refs[len(shares) :]
    row_ref, unit_ref, col_ref, before_ref, out_ref, sum_ref, edge_ref = refs
    after = my_core() == (1 if far else 0)
    keep = meet_ref[0, 0, 0]
    behind = shares[0] * BLOCK
    note = got[0][behind : behind + NOTE, :LANES].astype(jnp.float32)[0:1, :]
    lane = lax.broadcasted_iota(jnp.int32, (1, LANES), 1)
    held = [jnp.sum(jnp.where(lane == k, note, 0.0)).astype(jnp.int32) for k in range(4)]
    peak_row = jnp.where(after, held[0], peak_ref[0, keep, 0])
    peak_col = jnp.where(after, held[1], peak_ref[0, keep, 1])
    valid = jnp.where(after, held[2], valid_ref[0, keep])
    kind = jnp.where(after, 2, 0)
    side = jnp.where(after, held[3], keep)
    start = jnp.where(after, BATCHES * BLOCK, 0)
    sign = jnp.where(after, -1.0, 1.0)
    cross_into(sum_ref, edge_ref, batches_of([rest_ref], [BATCHES], start), batches_of(got, shares), sign)
    z = scores_of(sum_ref, edge_ref, row_ref, unit_ref, col_ref, peak_row, peak_col)
    total = before_ref[...] + node_row(z, peak_row, peak_col, valid, kind, side)
    out_ref[...] = jnp.broadcast_to(total, (1, LANES)) if not far else jnp.broadcast_to(
        total[None], out_ref.shape
    )


def relax_kernel(all_ref, scores_ref, positions_ref, hold_ref):
    sec, strip = lax.axis_index("sec"), lax.axis_index("strip")
    strips = 4
    lane = lax.broadcasted_iota(jnp.int32, (8, LANES), 1)
    row = lax.broadcasted_iota(jnp.int32, (8, LANES), 0)
    seat = lane % 64
    blocks = [all_ref[t * 64 : (t + 1) * 64, :] for t in range(strips)]
    joined = (blocks[0] + blocks[1]) + (blocks[2] + blocks[3])
    turned = jnp.concatenate([joined, jnp.zeros((64, LANES), jnp.float32)], axis=0).T

    def field(n):
        return turned[8 * n : 8 * n + 8]

    def both(low, high):
        return jnp.where(lane < 64, low, pltpu.roll(high, 64, 1))

    def first(n):
        return field(n) + jnp.where(lane == 0, 0.0, pltpu.roll(field(6 + n), 1, 1))

    w_a = jnp.where(lane == 0, 0.0, first(0))
    w_a, w_b = both(w_a, w_a), both(field(3), field(3))
    o_a = both(first(1), first(2))
    o_b = both(field(4), field(5))
    drift_a = jnp.sum(w_a * o_a, axis=0, keepdims=True) / (
        jnp.sum(w_a, axis=0, keepdims=True) + 1.0
    )
    drift_b = jnp.sum(w_b * o_b, axis=0, keepdims=True) / (
        jnp.sum(w_b, axis=0, keepdims=True) + 1.0
    )
    drift_a = jnp.broadcast_to(drift_a, (8, LANES))
    drift_b = jnp.broadcast_to(drift_b, (8, LANES))
    run = drift_a + drift_b
    for shift in (1, 2, 4, 8, 16, 32):
        run = run + jnp.where(seat >= shift, pltpu.roll(run, shift, 1), 0.0)
    p_b = run
    p_a = run - drift_b

    def links(p):
        left = jnp.where(row > 0, pltpu.roll(p, 1, 0), p)
        right = jnp.where(row < 7, pltpu.roll(p, 7, 0), p)
        return (p - left) + (p - right)

    w_next = pltpu.roll(w_a, LANES - 1, 1)
    o_next = pltpu.roll(o_a, LANES - 1, 1)
    for _ in range(ITERS):
        before = pltpu.roll(p_b, 1, 1)
        after = pltpu.roll(p_a, LANES - 1, 1)
        e_a = w_a * (p_a - before - o_a)
        e_b = w_b * (p_b - p_a - o_b)
        e_next = w_next * (after - p_b - o_next)
        n_a = p_a - STEP_SIZE * (e_a - e_b + KAPPA * links(p_a))
        n_b = p_b - STEP_SIZE * (e_b - e_next + KAPPA * links(p_b))
        p_a, p_b = n_a, n_b
    for s, p in enumerate((p_a, p_b)):
        first = jnp.sum(jnp.where(lane == sec, p, 0.0), axis=1, keepdims=True)
        other = jnp.sum(jnp.where(lane == sec + 64, p, 0.0), axis=1, keepdims=True)
        hold_ref[s] = jnp.where(lane == 0, first, other)
        for i in range(2):
            positions_ref[s, i : i + 1, :] = hold_ref[s, pl.ds(2 * strip + i, 1), :][:, :2]
    own = all_ref[pl.ds(strip * 64 + sec, 1), :]
    earlier = all_ref[pl.ds(strip * 64 + jnp.maximum(sec - 1, 0), 1), :]
    earlier = jnp.where(sec > 0, earlier, 0.0)
    for i in range(2):
        shift = LANES - SCORES - 5 * i
        value = pltpu.roll(own, shift, 1) + pltpu.roll(earlier, shift - 20, 1)
        scores_ref[0, i : i + 1, :] = value[:, :5]
        scores_ref[1, i : i + 1, :] = pltpu.roll(own, shift - 10, 1)[:, :5]


def sent_place(n, meet_ref, far):
    up = (my_core() == 1) == far
    return jnp.where(up, 1, 0), jnp.where(up, 0, 1 - meet_ref[0, 0, 0]), n


def sent_guess(far):
    up = (my_core() == 1) == far
    return (jnp.where(up, 1, 0), 0), (0, 1)


def rest_place(n, meet_ref):
    late = n // BATCHES
    return late, jnp.where(late == 0, meet_ref[0, 0, 0], 1), n % BATCHES


def body(features, intersection, peak_offsets, node_valid):
    secs, strips = lax.axis_size("sec"), lax.axis_size("strip")
    columns, rows = (jnp.asarray(t) for t in tables())
    row_phase, unit_phase, col_phase = (jnp.asarray(t) for t in phase_tables())
    integers = (intersection, peak_offsets, node_valid)

    def swap(first):
        pairs = [(i, i + 1) for i in range(first, secs - 1, 2)]
        return pairs + [(b, a) for a, b in pairs]

    sent_far, got_far = [], []
    for part, share in enumerate(FAR):
        begin = sum(FAR[:part])
        sent = spectra(
            features, integers, columns, rows,
            lambda n, meet, begin=begin: sent_place(begin + n, meet, True),
            functools.partial(sent_guess, far=True), begin, (share,), SPARE[part : part + 1],
            0 if part == 0 else None, 50, tuple(sent_far[-1:]),
        )
        sent_far.append(sent[0])
        got_far.append(lax.ppermute(sent[0], "sec", swap(1)))

    def last_place(n, meet):
        if isinstance(n, int) and n < BATCHES:
            return sent_place(n, meet, False)
        return rest_place(n - BATCHES, meet)

    *sent_near, rest = spectra(
        features, integers, columns, rows, last_place,
        functools.partial(sent_guess, far=False), 0,
        NEAR + (2 * BATCHES,), (1,) + (0,) * len(NEAR), 0, 44, tuple(sent_far[-1:]),
    )
    got_near = [lax.ppermute(part, "sec", swap(0)) for part in sent_near]

    smem = pl.BlockSpec(memory_space=pltpu.SMEM)
    vmem = pl.BlockSpec(memory_space=pltpu.VMEM)
    row_shape = jax.ShapeDtypeStruct((1, LANES), jnp.float32)

    def call(kernel, in_specs, out_shape, pairs, *args):
        lead = (2,) if pairs == 2 else ()
        return pl.pallas_call(
            kernel,
            in_specs=in_specs,
            out_specs=vmem,
            out_shape=out_shape,
            scratch_shapes=[
                pltpu.VMEM(lead + (2, WIDTH, LANES), jnp.float32),
                pltpu.VMEM(lead + (2, 8, LANES), jnp.float32),
            ],
            compiler_params=pltpu.CompilerParams(vmem_limit_bytes=16 * 1024 * 1024),
            cost_estimate=pl.CostEstimate(
                flops=1, bytes_accessed=1, transcendentals=0
            ),
        )(*args)

    phases = (row_phase, unit_phase, col_phase)
    local = call(
        local_kernel, [smem] * 3 + [vmem] * (len(FAR) + len(NEAR) + 4), row_shape, 2,
        *integers, *sent_far, *sent_near, rest, *phases,
    )
    near = call(
        functools.partial(met_kernel, far=False), [smem] * 3 + [vmem] * (len(NEAR) + 5), row_shape, 1,
        *integers, rest, *got_near, *phases, local,
    )
    message = call(
        functools.partial(met_kernel, far=True), [smem] * 3 + [vmem] * (len(FAR) + 5),
        jax.ShapeDtypeStruct((secs * strips, 1, LANES), jnp.float32), 1,
        *integers, rest, *got_far, *phases, near,
    )

    gathered = lax.all_to_all(message, ("strip", "sec"), 0, 0).reshape(strips, secs, LANES)
    if secs < 64:
        gathered = jnp.pad(gathered, ((0, 0), (0, 64 - secs), (0, 0)))
    gathered = gathered.reshape(strips * 64, LANES)
    scores, positions = pl.pallas_call(
        relax_kernel,
        in_specs=[vmem],
        out_specs=[vmem, vmem],
        out_shape=[
            jax.ShapeDtypeStruct((2, 2, 5), jnp.float32),
            jax.ShapeDtypeStruct((2, 2, 2), jnp.float32),
        ],
        scratch_shapes=[pltpu.VMEM((2, 8, LANES), jnp.float32)],
        compiler_params=pltpu.CompilerParams(vmem_limit_bytes=4 * 1024 * 1024),
    )(gathered)
    return scores, positions


def solution(mesh):
    placed = (
        P("sec", "strip", None, None, None),
        P("sec", "strip", None),
        P("sec", "strip", None),
        P("sec", "strip"),
    )
    return jax.shard_map(
        body,
        mesh=mesh,
        in_specs=placed,
        out_specs=(P("sec", "strip", None), P("sec", "strip", None)),
        check_vma=False,
    )
```

```python
import functools
import math

import jax
import jax.numpy as jnp
import ml_dtypes
import numpy as np
from jax import lax
from jax.experimental import pallas as pl
from jax.experimental.pallas import tpu as pltpu
from jax.sharding import PartitionSpec as P

ITERS = 8
KAPPA = 1.0
STEP_SIZE = 0.2
UNIT_SCALE = 0.125

WIDTH = 160
HALF = 80
LANES = 128
BATCH = 8
GROUPS = 5
PACKED = GROUPS * LANES
CHANNELS = 32
BATCHES = CHANNELS // BATCH
REACH = 13
BLOCK = 2 * WIDTH
CROSS_UNROLL = 10
SCORES = 72
PER_STEP = 2
FAR = (2, 2)
NEAR = (1, 1, 2)
SPARE = (2, 1)
NOTE = 16

SHIFTS = [(HALF * i) % LANES for i in range(BATCH)]
PIECES = [
    [(80, 0), (128, 1)],
    [(32, 1), (112, 2), (128, 3)],
    [(64, 3), (128, 4)],
    [(16, 4), (96, 5), (128, 6)],
    [(48, 6), (128, 7)],
]
STARTS = [[0, 80], [32, 112], [64], [16, 96], [48]]
ROW_FREQ = np.concatenate([np.arange(HALF), [HALF], -np.arange(1, HALF)])


def angle(product):
    return 2.0 * math.pi / WIDTH * (product % WIDTH)


def tables():
    counter = np.arange(WIDTH)
    angles = angle(counter[:, None] * counter[None, :])
    cosine, sine = np.cos(angles), np.sin(angles)
    cos_part = cosine[:HALF]
    sin_part = np.concatenate([cosine[HALF : HALF + 1], sine[1:HALF]], axis=0)
    rows = np.concatenate([cos_part, sin_part], axis=0)
    columns = np.zeros((WIDTH, 2 * LANES))
    columns[:, :HALF] = cos_part.T
    columns[:, LANES : LANES + HALF] = sin_part.T
    return columns.astype(ml_dtypes.bfloat16), rows.astype(ml_dtypes.bfloat16)


def phase_tables():
    peaks = np.arange(-REACH, REACH + 1)
    rows = np.zeros((WIDTH, LANES))
    a = angle(ROW_FREQ[:, None] * peaks[None, :])
    rows[:, : len(peaks)] = np.cos(a)
    rows[:, 64 : 64 + len(peaks)] = np.sin(a)
    unit = np.zeros((2, WIDTH, LANES))
    unit[0] = np.cos(angle(ROW_FREQ))[:, None]
    unit[1] = np.sin(angle(ROW_FREQ))[:, None]
    columns = np.zeros((4, 32, LANES))
    low = np.arange(HALF)
    high = low.copy()
    high[0] = HALF
    for h, freq in enumerate((low, high)):
        b = angle(peaks[:, None] * freq[None, :])
        columns[2 * h, : len(peaks), :HALF] = np.cos(b)
        columns[2 * h + 1, : len(peaks), :HALF] = np.sin(b)
    return rows.astype(np.float32), unit.astype(np.float32), columns.astype(np.float32)


def transform(image, columns_ref, rows_ref, packed_ref, store):
    lane2 = lax.broadcasted_iota(jnp.int32, (1, 2 * LANES), 1) % LANES
    halves = {}

    def half(i):
        halves[i] = jnp.dot(image(i), columns_ref[i], preferred_element_type=jnp.float32)

    def pack(group):
        pieces = PIECES[group]
        value = halves[pieces[-1][1]]
        for end, i in pieces[-2::-1]:
            value = jnp.where(lane2 < end, halves[i], value)
        packed_ref[:, group * 2 * LANES : (group + 1) * 2 * LANES] = value.astype(jnp.bfloat16)

    lane = lax.broadcasted_iota(jnp.int32, (1, LANES), 1)
    edge = lax.broadcasted_iota(jnp.int32, (16, LANES), 0) == 0

    def finish(group):
        whole = jnp.dot(
            rows_ref[...],
            packed_ref[:, group * 2 * LANES : (group + 1) * 2 * LANES],
            preferred_element_type=jnp.float32,
        )
        first = lane == STARTS[group][0]
        for start in STARTS[group][1:]:
            first = first | (lane == start)
        cc, cs = whole[:HALF, :LANES], whole[:HALF, LANES:]
        sc, ss = whole[HALF:, :LANES], whole[HALF:, LANES:]
        ss0 = jnp.where(first, 0.0, ss)
        cs0 = jnp.where(first, 0.0, cs)
        values = [
            (0, 0, cc - ss0, cc),
            (0, 1, jnp.where(first, cs, cc + ss0), jnp.where(first, cs, sc)),
            (1, 0, -(cs0 + sc), jnp.where(first, -sc, -cs)),
            (1, 1, jnp.where(first, ss, sc - cs0), jnp.where(first, ss, -ss)),
        ]
        for c, h, value, fixed in values:
            top = jnp.where(edge, fixed[:16], value[:16]).astype(jnp.bfloat16)
            store(c, h * HALF, 16, group, top)
            store(c, h * HALF + 16, HALF - 16, group, value[16:].astype(jnp.bfloat16))

    half(0)
    half(1)
    pack(0)
    half(2)
    half(3)
    pack(1)
    finish(0)
    half(4)
    pack(2)
    finish(1)
    half(5)
    half(6)
    pack(3)
    finish(2)
    half(7)
    pack(4)
    finish(3)
    finish(4)


def spectra_kernel(*refs, where, guess, begin, parts, noted, after):
    count = sum(parts)
    meet_in, peaks_in, valids_in, images_ref, columns_in, rows_in, *refs = refs
    refs = refs[1:] if after else refs
    outs, refs = refs[: len(parts)], refs[len(parts) :]
    held_ref, packed_ref, base_ref, columns_ref, rows_ref, *refs = refs
    meet_ref, peaks_ref, valids_ref, sems, other_sems = refs

    def fetch(n):
        section, patch, batch = where(n, meet_ref)
        return pltpu.make_async_copy(
            images_ref.at[section, patch, pl.ds(batch * BATCH, BATCH)], held_ref.at[n], sems.at[n]
        )

    meet = pltpu.make_async_copy(meet_in, meet_ref, other_sems.at[0])
    meet.start()
    others = [
        pltpu.make_async_copy(columns_in, base_ref, other_sems.at[1]),
        pltpu.make_async_copy(rows_in, rows_ref, other_sems.at[2]),
    ]
    if noted is not None:
        others.append(pltpu.make_async_copy(peaks_in, peaks_ref, other_sems.at[3]))
        others.append(pltpu.make_async_copy(valids_in, valids_ref, other_sems.at[4]))
    for other in others:
        other.start()
    guesses = [
        pltpu.make_async_copy(
            images_ref.at[section, patch, pl.ds(begin * BATCH, BATCH)], held_ref.at[slot], sems.at[slot]
        )
        for (section, patch), slot in zip(guess(), (0, count))
    ]
    for copy in guesses:
        copy.start()
    meet.wait()
    for n in range(1, count):
        fetch(n).start()
    for other in others:
        other.wait()
    for g in range(2):
        lanes = slice(g * LANES, (g + 1) * LANES)
        base = base_ref[:, lanes].astype(jnp.float32)
        for i, shift in enumerate(SHIFTS):
            moved = pltpu.roll(base, shift, 1) if shift else base
            columns_ref[i, :, lanes] = moved.astype(jnp.bfloat16)

    for copy in guesses:
        copy.wait()
    began = jnp.where(where(0, meet_ref)[1] == guess()[0][1], 0, count)

    def one(n, slot, out_ref, base):
        static = isinstance(n, int)
        if static and n > 0:
            fetch(n).wait()
        elif not static:
            pl.when(n > 0)(lambda: fetch(n).wait())
        at_held = jnp.where(n == 0, began, n)

        def store(c, row, size, group, value):
            at = pl.multiple_of(base + c * WIDTH + row, 16)
            out_ref[pl.ds(at, size), group * LANES : (group + 1) * LANES] = value

        transform(lambda i: held_ref[at_held, i], columns_ref, rows_ref, packed_ref.at[slot], store)

    first = 0
    for out_ref, size in zip(outs, parts):
        if size <= PER_STEP:
            for n in range(size):
                one(first + n, (first + n) % PER_STEP, out_ref, n * BLOCK)
        else:

            def step(k, carry, out_ref=out_ref, first=first):
                for slot in range(PER_STEP):
                    n = k * PER_STEP + slot
                    one(first + n, slot, out_ref, n * BLOCK)
                return carry

            lax.fori_loop(0, size // PER_STEP, step, 0)
        first += size

    if noted is not None:
        give = 1 - meet_ref[0, 0, 0]
        lane = lax.broadcasted_iota(jnp.int32, (NOTE, PACKED), 1)
        note = jnp.zeros((NOTE, PACKED), jnp.float32)
        values = [peaks_ref[0, give, 0], peaks_ref[0, give, 1], valids_ref[0, give], give]
        for k, value in enumerate(values):
            note = jnp.where(lane == k, value.astype(jnp.float32), note)
        behind = parts[noted] * BLOCK
        outs[noted][behind : behind + NOTE, :] = note.astype(jnp.bfloat16)


def spectra(features, integers, columns, rows, where, guess, begin, parts, spare, noted, limit, after=()):
    count = sum(parts)
    vmem = pl.BlockSpec(memory_space=pltpu.VMEM)
    anywhere = pl.BlockSpec(memory_space=pl.ANY)
    hbm = pl.BlockSpec(memory_space=pltpu.HBM)
    return pl.pallas_call(
        functools.partial(
            spectra_kernel, where=where, guess=guess, begin=begin, parts=parts, noted=noted,
            after=bool(after),
        ),
        in_specs=[hbm] * 6 + [anywhere] * len(after),
        out_specs=[vmem] * len(parts),
        out_shape=[
            jax.ShapeDtypeStruct((n * BLOCK + NOTE * k, PACKED), jnp.bfloat16)
            for n, k in zip(parts, spare)
        ],
        scratch_shapes=[
            pltpu.VMEM((count + 1, BATCH, WIDTH, WIDTH), jnp.bfloat16),
            pltpu.VMEM((PER_STEP, WIDTH, 2 * PACKED), jnp.bfloat16),
            pltpu.VMEM(columns.shape, jnp.bfloat16),
            pltpu.VMEM((BATCH,) + columns.shape, jnp.bfloat16),
            pltpu.VMEM(rows.shape, jnp.bfloat16),
            pltpu.SMEM(integers[0].shape, jnp.int32),
            pltpu.SMEM(integers[1].shape, jnp.int32),
            pltpu.SMEM(integers[2].shape, jnp.int32),
            pltpu.SemaphoreType.DMA((count + 1,)),
            pltpu.SemaphoreType.DMA((5,)),
        ],
        compiler_params=pltpu.CompilerParams(vmem_limit_bytes=limit * 1024 * 1024),
        cost_estimate=pl.CostEstimate(
            flops=count * BATCH * 2 * 2 * WIDTH * WIDTH,
            bytes_accessed=count * BATCH * 1400,
            transcendentals=0,
        ),
    )(*(pltpu.with_memory_space_constraint(a, pltpu.HBM) for a in (*integers, features, columns, rows)), *after)


def my_core():
    return lax.axis_index("sec") % 2


def gather_windows(g):
    lane = lax.broadcasted_iota(jnp.int32, (1, LANES), 1)
    low = lane < 80
    windows = [
        (80, jnp.where(low, g[1], g[0])),
        (32, g[1]),
        (112, jnp.where(lane < 112, g[2], g[1])),
        (64, jnp.where(lane < 64, g[3], g[2])),
        (16, g[3]),
        (96, jnp.where(lane < 96, g[4], g[3])),
        (48, g[4]),
    ]
    total = g[0]
    for shift, value in windows:
        total = total + pltpu.roll(value, LANES - shift, 1)
    return total


def cross_into(sum_ref, edge_ref, own, near, sign):
    def load(side, n, c, start, lanes):
        ref, base = side[n]
        at = pl.multiple_of(base + c * WIDTH + start, 16)
        return ref[pl.ds(at, 16), lanes].astype(jnp.float32)

    def step(k, carry):
        start = pl.multiple_of(k * 16, 16)
        reals, imags = [], []
        for group in range(GROUPS):
            lanes = slice(group * LANES, (group + 1) * LANES)
            real = imag = None
            for n in range(BATCHES):
                own_re, own_im = (load(own, n, c, start, lanes) for c in range(2))
                near_re, near_im = (load(near, n, c, start, lanes) for c in range(2))
                re = own_re * near_re + own_im * near_im
                im = own_re * near_im - own_im * near_re
                real = re if real is None else real + re
                imag = im if imag is None else imag + im
            reals.append(real)
            imags.append(imag)
        sum_ref[0, pl.ds(start, 16), :] = gather_windows(reals)
        sum_ref[1, pl.ds(start, 16), :] = sign * gather_windows(imags)
        return carry

    lax.fori_loop(0, WIDTH // 16, step, 0, unroll=CROSS_UNROLL)
    for h in range(2):
        boths = []
        for group in range(GROUPS):
            lanes = slice(group * LANES, (group + 1) * LANES)
            both = None
            for n in range(BATCHES):
                ii = load(own, n, 1, h * HALF, lanes) * load(near, n, 1, h * HALF, lanes)
                both = ii if both is None else both + ii
            boths.append(both[:8])
        edge_ref[h] = gather_windows(boths)


def scores_of(sum_ref, edge_ref, row_ref, unit_ref, col_ref, peak_row, peak_col):
    lane = lax.broadcasted_iota(jnp.int32, (1, LANES), 1)
    damp = WIDTH * WIDTH * math.sqrt(CHANNELS)
    sums = {}
    moved = pltpu.roll(row_ref[...], (LANES - REACH) - peak_row, 1)
    for h in range(2):
        rows = slice(h * HALF, (h + 1) * HALF)
        real, imag = sum_ref[0, rows, :], sum_ref[1, rows, :]
        inverse = 1.0 / (jnp.sqrt(real * real + imag * imag) + damp)
        white_re, white_im = real * inverse, imag * inverse
        ii = edge_ref[h][0:1, :]
        rr = real[0:1, :] - ii
        z_rr = 0.5 * rr / (jnp.abs(rr) + damp)
        z_ii = 0.5 * ii / (jnp.abs(ii) + damp)
        stays, goes = (z_rr, z_ii) if h == 0 else (z_ii, z_rr)
        corner = (lax.broadcasted_iota(jnp.int32, (8, LANES), 0) == 0) & (
            lax.broadcasted_iota(jnp.int32, (8, LANES), 1) == 0
        )
        white_re = jnp.concatenate(
            [jnp.where(corner, jnp.broadcast_to(stays, (8, LANES)), white_re[:8]), white_re[8:]], 0
        )
        white_im = jnp.concatenate([jnp.where(corner, 0.0, white_im[:8]), white_im[8:]], 0)
        cos, sin = moved[rows, 0:1], moved[rows, 64:65]
        turned_re = white_re * cos - white_im * sin
        turned_im = white_re * sin + white_im * cos
        unit_cos, unit_sin = unit_ref[0, rows, :], unit_ref[1, rows, :]
        add = lambda x: jnp.sum(x, axis=0, keepdims=True)
        plain_re, plain_im = add(turned_re), add(turned_im)
        cos_re, cos_im = add(turned_re * unit_cos), add(turned_im * unit_cos)
        sin_re, sin_im = add(turned_re * unit_sin), add(turned_im * unit_sin)
        sums[h] = [
            (plain_re, plain_im),
            (cos_re + sin_im, cos_im - sin_re),
            (cos_re - sin_im, cos_im + sin_re),
        ]
        extra = jnp.where(lane == 0, goes, 0.0)
        for a in range(3):
            turn = moved[HALF : HALF + 1, 0:1] * (1.0 if a == 0 else -1.0) if h == 0 else 1.0
            sums[h][a] = (sums[h][a][0] + extra * turn, sums[h][a][1])
    out = []
    for a, b in ((0, 0), (1, 0), (2, 0), (0, -1), (0, 1)):
        total = None
        for h in range(2):
            cos = col_ref[2 * h, pl.ds(peak_col + (REACH + b), 1), :]
            sin = col_ref[2 * h + 1, pl.ds(peak_col + (REACH + b), 1), :]
            term = sums[h][a][0] * cos - sums[h][a][1] * sin
            total = term if total is None else total + term
        out.append(jnp.sum(total, axis=1, keepdims=True) * (4.0 / WIDTH))
    return out


def node_row(z, peak_row, peak_col, valid, kind, side):
    lane = lax.broadcasted_iota(jnp.int32, (1, LANES), 1)
    wide = [jnp.broadcast_to(value, (1, LANES)) for value in z]
    spread_row = jnp.abs(wide[1]) + jnp.abs(wide[0]) + jnp.abs(wide[2]) + 1.0
    spread_col = jnp.abs(wide[3]) + jnp.abs(wide[0]) + jnp.abs(wide[4]) + 1.0
    off_row = UNIT_SCALE * (
        peak_row.astype(jnp.float32) + 0.5 * (wide[2] - wide[1]) / spread_row
    )
    off_col = UNIT_SCALE * (
        peak_col.astype(jnp.float32) + 0.5 * (wide[4] - wide[3]) / spread_col
    )
    weight = valid.astype(jnp.float32) * (1.0 + jnp.tanh(wide[0]))
    first = 24 * kind + 2 * lax.axis_index("strip") + side
    row = jnp.zeros((1, LANES), jnp.float32)
    for n, value in enumerate([weight, off_row, off_col]):
        row = jnp.where(lane == first + 8 * n, value, row)
    for n, value in enumerate(wide):
        row = jnp.where(lane == SCORES + 10 * kind + 5 * side + n, value, row)
    return row


def batches_of(refs, shares, start=0):
    return [(ref, start + n * BLOCK) for ref, share in zip(refs, shares) for n in range(share)]


def local_kernel(meet_ref, peak_ref, valid_ref, *refs):
    far = batches_of(refs[: len(FAR)], FAR)
    near = batches_of(refs[len(FAR) : len(FAR) + len(NEAR)], NEAR)
    rest_ref, row_ref, unit_ref, col_ref, out_ref, sum_ref, edge_ref = refs[len(FAR) + len(NEAR) :]
    first = batches_of([rest_ref], [BATCHES])
    second = batches_of([rest_ref], [BATCHES], BATCHES * BLOCK)
    core = my_core()
    same = meet_ref[1, 0, 0] == 1 - meet_ref[0, 0, 0]

    @pl.when(same)
    def _():
        sign = jnp.where(core == 1, 1.0, -1.0)
        cross_into(sum_ref.at[0], edge_ref.at[0], far, near, sign)
        cross_into(sum_ref.at[1], edge_ref.at[1], second, first, 1.0)

    def apart(patch, given):
        cross_into(sum_ref.at[0], edge_ref.at[0], patch, first, 1.0)
        cross_into(sum_ref.at[1], edge_ref.at[1], second, given, 1.0)

    pl.when(jnp.logical_not(same) & (core == 1))(lambda: apart(far, near))
    pl.when(jnp.logical_not(same) & (core == 0))(lambda: apart(near, far))

    total = jnp.zeros((1, LANES), jnp.float32)
    for n in range(2):
        peak = peak_ref[1, n, 0], peak_ref[1, n, 1]
        z = scores_of(sum_ref.at[n], edge_ref.at[n], row_ref, unit_ref, col_ref, *peak)
        total = total + node_row(z, *peak, valid_ref[1, n], 1, n)
    out_ref[...] = total


def met_row(integers, rest_ref, got, phases, sum_ref, edge_ref, far):
    meet_ref, peak_ref, valid_ref = integers
    shares = FAR if far else NEAR
    after = my_core() == (1 if far else 0)
    keep = meet_ref[0, 0, 0]
    behind = shares[0] * BLOCK
    note = got[0][behind : behind + NOTE, :LANES].astype(jnp.float32)[0:1, :]
    lane = lax.broadcasted_iota(jnp.int32, (1, LANES), 1)
    held = [jnp.sum(jnp.where(lane == k, note, 0.0)).astype(jnp.int32) for k in range(4)]
    peak_row = jnp.where(after, held[0], peak_ref[0, keep, 0])
    peak_col = jnp.where(after, held[1], peak_ref[0, keep, 1])
    valid = jnp.where(after, held[2], valid_ref[0, keep])
    kind = jnp.where(after, 2, 0)
    side = jnp.where(after, held[3], keep)
    start = jnp.where(after, BATCHES * BLOCK, 0)
    sign = jnp.where(after, -1.0, 1.0)
    cross_into(sum_ref, edge_ref, batches_of([rest_ref], [BATCHES], start), batches_of(got, shares), sign)
    z = scores_of(sum_ref, edge_ref, *phases, peak_row, peak_col)
    return node_row(z, peak_row, peak_col, valid, kind, side)


def met_kernel(meet_ref, peak_ref, valid_ref, rest_ref, *refs):
    near, refs = refs[: len(NEAR)], refs[len(NEAR) :]
    far, refs = refs[: len(FAR)], refs[len(FAR) :]
    row_ref, unit_ref, col_ref, before_ref, out_ref, sum_ref, edge_ref = refs
    integers, phases = (meet_ref, peak_ref, valid_ref), (row_ref, unit_ref, col_ref)
    total = before_ref[...]
    for n, got in enumerate((near, far)):
        total = total + met_row(
            integers, rest_ref, got, phases, sum_ref.at[n], edge_ref.at[n], n == 1
        )
    out_ref[...] = jnp.broadcast_to(total[None], out_ref.shape)


def relax_kernel(all_ref, scores_ref, positions_ref, hold_ref):
    sec, strip = lax.axis_index("sec"), lax.axis_index("strip")
    strips = 4
    lane = lax.broadcasted_iota(jnp.int32, (8, LANES), 1)
    row = lax.broadcasted_iota(jnp.int32, (8, LANES), 0)
    seat = lane % 64
    blocks = [all_ref[t * 64 : (t + 1) * 64, :] for t in range(strips)]
    joined = (blocks[0] + blocks[1]) + (blocks[2] + blocks[3])
    turned = jnp.concatenate([joined, jnp.zeros((64, LANES), jnp.float32)], axis=0).T

    def field(n):
        return turned[8 * n : 8 * n + 8]

    def both(low, high):
        return jnp.where(lane < 64, low, pltpu.roll(high, 64, 1))

    def first(n):
        return field(n) + jnp.where(lane == 0, 0.0, pltpu.roll(field(6 + n), 1, 1))

    w_a = jnp.where(lane == 0, 0.0, first(0))
    w_a, w_b = both(w_a, w_a), both(field(3), field(3))
    o_a = both(first(1), first(2))
    o_b = both(field(4), field(5))
    drift_a = jnp.sum(w_a * o_a, axis=0, keepdims=True) / (
        jnp.sum(w_a, axis=0, keepdims=True) + 1.0
    )
    drift_b = jnp.sum(w_b * o_b, axis=0, keepdims=True) / (
        jnp.sum(w_b, axis=0, keepdims=True) + 1.0
    )
    drift_a = jnp.broadcast_to(drift_a, (8, LANES))
    drift_b = jnp.broadcast_to(drift_b, (8, LANES))
    run = drift_a + drift_b
    for shift in (1, 2, 4, 8, 16, 32):
        run = run + jnp.where(seat >= shift, pltpu.roll(run, shift, 1), 0.0)
    p_b = run
    p_a = run - drift_b

    def links(p):
        left = jnp.where(row > 0, pltpu.roll(p, 1, 0), p)
        right = jnp.where(row < 7, pltpu.roll(p, 7, 0), p)
        return (p - left) + (p - right)

    w_next = pltpu.roll(w_a, LANES - 1, 1)
    o_next = pltpu.roll(o_a, LANES - 1, 1)
    for _ in range(ITERS):
        before = pltpu.roll(p_b, 1, 1)
        after = pltpu.roll(p_a, LANES - 1, 1)
        e_a = w_a * (p_a - before - o_a)
        e_b = w_b * (p_b - p_a - o_b)
        e_next = w_next * (after - p_b - o_next)
        n_a = p_a - STEP_SIZE * (e_a - e_b + KAPPA * links(p_a))
        n_b = p_b - STEP_SIZE * (e_b - e_next + KAPPA * links(p_b))
        p_a, p_b = n_a, n_b
    for s, p in enumerate((p_a, p_b)):
        first = jnp.sum(jnp.where(lane == sec, p, 0.0), axis=1, keepdims=True)
        other = jnp.sum(jnp.where(lane == sec + 64, p, 0.0), axis=1, keepdims=True)
        hold_ref[s] = jnp.where(lane == 0, first, other)
        for i in range(2):
            positions_ref[s, i : i + 1, :] = hold_ref[s, pl.ds(2 * strip + i, 1), :][:, :2]
    own = all_ref[pl.ds(strip * 64 + sec, 1), :]
    earlier = all_ref[pl.ds(strip * 64 + jnp.maximum(sec - 1, 0), 1), :]
    earlier = jnp.where(sec > 0, earlier, 0.0)
    for i in range(2):
        shift = LANES - SCORES - 5 * i
        value = pltpu.roll(own, shift, 1) + pltpu.roll(earlier, shift - 20, 1)
        scores_ref[0, i : i + 1, :] = value[:, :5]
        scores_ref[1, i : i + 1, :] = pltpu.roll(own, shift - 10, 1)[:, :5]


def sent_place(n, meet_ref, far):
    up = (my_core() == 1) == far
    return jnp.where(up, 1, 0), jnp.where(up, 0, 1 - meet_ref[0, 0, 0]), n


def sent_guess(far):
    up = (my_core() == 1) == far
    return (jnp.where(up, 1, 0), 0), (0, 1)


def rest_place(n, meet_ref):
    late = n // BATCHES
    return late, jnp.where(late == 0, meet_ref[0, 0, 0], 1), n % BATCHES


def body(features, intersection, peak_offsets, node_valid):
    secs, strips = lax.axis_size("sec"), lax.axis_size("strip")
    columns, rows = (jnp.asarray(t) for t in tables())
    row_phase, unit_phase, col_phase = (jnp.asarray(t) for t in phase_tables())
    integers = (intersection, peak_offsets, node_valid)

    def swap(first):
        pairs = [(i, i + 1) for i in range(first, secs - 1, 2)]
        return pairs + [(b, a) for a, b in pairs]

    sent_far, got_far = [], []
    for part, share in enumerate(FAR):
        begin = sum(FAR[:part])
        sent = spectra(
            features, integers, columns, rows,
            lambda n, meet, begin=begin: sent_place(begin + n, meet, True),
            functools.partial(sent_guess, far=True), begin, (share,), SPARE[part : part + 1],
            0 if part == 0 else None, 50, tuple(sent_far[-1:]),
        )
        sent_far.append(sent[0])
        got_far.append(lax.ppermute(sent[0], "sec", swap(1)))

    def last_place(n, meet):
        if isinstance(n, int) and n < BATCHES:
            return sent_place(n, meet, False)
        return rest_place(n - BATCHES, meet)

    *sent_near, rest = spectra(
        features, integers, columns, rows, last_place,
        functools.partial(sent_guess, far=False), 0,
        NEAR + (2 * BATCHES,), (1,) + (0,) * len(NEAR), 0, 44, tuple(sent_far[-1:]),
    )
    got_near = [lax.ppermute(part, "sec", swap(0)) for part in sent_near]

    smem = pl.BlockSpec(memory_space=pltpu.SMEM)
    vmem = pl.BlockSpec(memory_space=pltpu.VMEM)
    row_shape = jax.ShapeDtypeStruct((1, LANES), jnp.float32)

    def call(kernel, in_specs, out_shape, pairs, *args):
        lead = (2,) if pairs == 2 else ()
        return pl.pallas_call(
            kernel,
            in_specs=in_specs,
            out_specs=vmem,
            out_shape=out_shape,
            scratch_shapes=[
                pltpu.VMEM(lead + (2, WIDTH, LANES), jnp.float32),
                pltpu.VMEM(lead + (2, 8, LANES), jnp.float32),
            ],
            compiler_params=pltpu.CompilerParams(vmem_limit_bytes=16 * 1024 * 1024),
            cost_estimate=pl.CostEstimate(
                flops=1, bytes_accessed=1, transcendentals=0
            ),
        )(*args)

    phases = (row_phase, unit_phase, col_phase)
    local = call(
        local_kernel, [smem] * 3 + [vmem] * (len(FAR) + len(NEAR) + 4), row_shape, 2,
        *integers, *sent_far, *sent_near, rest, *phases,
    )
    message = call(
        met_kernel, [smem] * 3 + [vmem] * (len(NEAR) + len(FAR) + 5),
        jax.ShapeDtypeStruct((secs * strips, 1, LANES), jnp.float32), 2,
        *integers, rest, *got_near, *got_far, *phases, local,
    )

    gathered = lax.all_to_all(message, ("strip", "sec"), 0, 0).reshape(strips, secs, LANES)
    if secs < 64:
        gathered = jnp.pad(gathered, ((0, 0), (0, 64 - secs), (0, 0)))
    gathered = gathered.reshape(strips * 64, LANES)
    scores, positions = pl.pallas_call(
        relax_kernel,
        in_specs=[vmem],
        out_specs=[vmem, vmem],
        out_shape=[
            jax.ShapeDtypeStruct((2, 2, 5), jnp.float32),
            jax.ShapeDtypeStruct((2, 2, 2), jnp.float32),
        ],
        scratch_shapes=[pltpu.VMEM((2, 8, LANES), jnp.float32)],
        compiler_params=pltpu.CompilerParams(vmem_limit_bytes=4 * 1024 * 1024),
    )(gathered)
    return scores, positions


def solution(mesh):
    placed = (
        P("sec", "strip", None, None, None),
        P("sec", "strip", None),
        P("sec", "strip", None),
        P("sec", "strip"),
    )
    return jax.shard_map(
        body,
        mesh=mesh,
        in_specs=placed,
        out_specs=(P("sec", "strip", None), P("sec", "strip", None)),
        check_vma=False,
    )
```
